512 devices in a mesh: atom: 16 (over x, y_lo, core), row: 8 (over z), col: 4 (over y_hi).
Axes of the slice: x: 4, y: 8 (y_hi: 4, y_lo: 2; y = y_hi * 2 + y_lo), z: 8, core: 2. Of those that a mesh axis runs over, the one named last changes fastest.
Arguments:
- codes: bfloat16 [128, 64, 2048], P('row', 'col', 'atom'), may hold values from -1.5 to 1.5
- image: bfloat16 [128, 64, 128], P('row', 'col'), may hold values from -6 to 6
- master: float32 [128, 7, 7, 2048], P(('row', 'col'), None, None, 'atom'), may hold values from -0.078125 to 0.078125
- moment: float32 [128, 7, 7, 2048], P(('row', 'col'), None, None, 'atom'), may hold values from -120 to 120
- second: float32 [128, 7, 7, 2048], P(('row', 'col'), None, None, 'atom'), may hold values from 100 to 4000
Outputs:
- new_codes: bfloat16 [128, 64, 2048], P('row', 'col', 'atom')
- new_dictionary: float32 [128, 7, 7, 2048], P(('row', 'col'), None, None, 'atom')
- new_moment: float32 [128, 7, 7, 2048], P(('row', 'col'), None, None, 'atom')
- new_second: float32 [128, 7, 7, 2048], P(('row', 'col'), None, None, 'atom')
The draws below stay inside these ranges and needn't reach their ends.
All inputs are finite; a program needn't handle non-finite values.
Results may differ from the reference program's by a relative error of at most 0.007.
Values may be sent and summed in bfloat16 or wider, within the bound.
A program may use at most 64 MiB of HBM per device.

```python
import math
import jax
import jax.numpy as jnp
from jax import lax

C = 128
K = 2048
FS = 7
NH = 128
NW = 64


def block_scale(stream_key, extent, shards, smallest, high):
    factor_of, own = 1.0, jax.random.fold_in(stream_key, 6)
    for axis_at, parts in shards:
        draws = jnp.exp(jax.random.uniform(jax.random.fold_in(own, axis_at), (parts,), jnp.float32, smallest / len(shards), high / len(shards)))
        factor_of = factor_of * jnp.repeat(draws, extent[axis_at] // parts).reshape([-1 if axis == axis_at else 1 for axis in range(len(extent))])
    return factor_of


def normal_values(rng, dims, spread, bound, pieces=(), dtype=jnp.bfloat16):
    factor_of = block_scale(rng, dims, pieces, -0.22, 0.18) if pieces else 1.0
    drawn = jax.random.normal(rng, dims, jnp.float32) * spread * factor_of
    return jnp.minimum(jnp.maximum(drawn, -bound), bound).astype(dtype)


def setup_inputs(seed: int = 0) -> dict:
    key_of = jax.random.split(jax.random.key(seed), 6)
    codes = normal_values(key_of[0], (NH, NW, K), 0.25, 1.5, ((0, 8), (1, 4), (2, 16)))
    image = normal_values(key_of[1], (NH, NW, C), 1.0, 6.0, ((0, 8), (1, 4)))
    master = normal_values(key_of[2], (C, FS, FS, K), (C * FS * FS) ** -0.5, 0.078125, ((0, 32), (3, 16)), jnp.float32)
    moment = normal_values(key_of[3], (C, FS, FS, K), 20.0, 120.0, ((0, 32), (3, 16)), jnp.float32)
    second = jnp.clip(jnp.exp(math.log(4000.0) - 3.6888795 * jax.random.uniform(key_of[4], (C, FS, FS, K), jnp.float32) ** block_scale(key_of[4], (C, FS, FS, K), ((0, 32), (3, 16)), -0.2, 0.2)), 100.0, 4000.0)
    return {"codes": codes, "image": image, "master": master, "moment": moment, "second": second}


first_fix = 0.9999734386011124
second_fix = 0.09520785288629038

def reference(codes, image, master, moment, second):
    rows_all, cols_all, atoms = codes.shape
    bands = image.shape[2]
    pixels = rows_all * cols_all
    filters = master.astype(jnp.bfloat16)
    zero = jnp.zeros((), jnp.int32)
    code_pad = jnp.pad(codes, ((3, 3), (3, 3), (0, 0)))

    def add_synth(tap_index, total):
        tap_row = (tap_index // FS).astype(jnp.int32)
        tap_col = (tap_index % FS).astype(jnp.int32)
        window = lax.dynamic_slice(code_pad, (tap_row, tap_col, zero), (rows_all, cols_all, atoms)).reshape(pixels, atoms)
        tap = lax.dynamic_slice(filters, (zero, tap_row, tap_col, zero), (bands, 1, 1, atoms)).reshape(bands, atoms)
        return total + jnp.dot(window, tap.T, preferred_element_type=jnp.float32)
    synth = lax.fori_loop(0, FS * FS, add_synth, jnp.zeros((pixels, bands), jnp.float32))
    resid = (synth - image.reshape(pixels, bands).astype(jnp.float32)).astype(jnp.bfloat16)
    resid_pad = jnp.pad(resid.reshape(rows_all, cols_all, bands), ((3, 3), (3, 3), (0, 0)))

    def add_both(tap_index, carry):
        back, grad = carry
        tap_row = (tap_index // FS).astype(jnp.int32)
        tap_col = (tap_index % FS).astype(jnp.int32)
        tap = lax.dynamic_slice(filters, (zero, tap_row, tap_col, zero), (bands, 1, 1, atoms)).reshape(bands, atoms)
        flipped = lax.dynamic_slice(resid_pad, (6 - tap_row, 6 - tap_col, zero), (rows_all, cols_all, bands)).reshape(pixels, bands)
        back = back + jnp.dot(flipped, tap, preferred_element_type=jnp.float32)
        window = lax.dynamic_slice(code_pad, (tap_row, tap_col, zero), (rows_all, cols_all, atoms)).reshape(pixels, atoms)
        term = lax.dot_general(resid, window, (((0,), (0,)), ((), ())), preferred_element_type=jnp.float32)
        grad = lax.dynamic_update_slice(grad, term.reshape(bands, 1, 1, atoms), (zero, tap_row, tap_col, zero))
        return (back, grad)
    back, grad = lax.fori_loop(0, FS * FS, add_both, (jnp.zeros((pixels, atoms), jnp.float32), jnp.zeros((bands, FS, FS, atoms), jnp.float32)))
    moved = codes.reshape(pixels, atoms).astype(jnp.float32) - 0.05 * back
    new_codes = (moved - jnp.clip(moved, -0.02, 0.02)).astype(jnp.bfloat16).reshape(rows_all, cols_all, atoms)
    new_moment = 0.9 * moment + 0.1 * grad
    new_second = 0.999 * second + 0.001 * grad * grad
    new_dictionary = master - 0.05 * (new_moment / first_fix) / (jnp.sqrt(new_second / second_fix) + 1e-08)
    return (new_codes, new_dictionary, new_moment, new_second)
```

```python
import jax
import jax.numpy as jnp
from jax import lax
from jax.experimental import pallas as pl
from jax.experimental.pallas import tpu as pltpu
from jax.sharding import PartitionSpec as P

MESH = pl.DeviceIdType.MESH
F32, BF16 = jnp.float32, jnp.bfloat16
first_fix = 0.9999734386011124
second_fix = 0.09520785288629038
ROWS, COLS, ATOMS = 8, 4, 16
TAPS = 7


def kernel(
    codes, image, master, moment, second,
    out_codes, out_dict, out_moment, out_second,
    x_buf, x7, f_buf, f_scr, m_buf, mo_buf, se_buf,
    img_in, img_out, img_got,
    pt, halo_out, halo_got, part_out, part_got,
    resid, edge_got, xr, xrb,
    g_out, g_got, p2, bk_out, bk_got, g_scr,
    in_sem, f_send, f_recv, c_send, c_recv, i_send, i_recv,
    h_send, h_recv, p_send, p_recv, r_send, r_recv, e_send, e_recv,
    g_send, g_recv, b_send, b_recv,
):
    r = lax.axis_index("row")
    q = lax.axis_index("col")
    t = lax.axis_index("atom")
    pair, half = t // 2, lax.rem(t, 2)

    def remote(src, dst, send, recv, who):
        return pltpu.make_async_remote_copy(
            src_ref=src, dst_ref=dst, send_sem=send, recv_sem=recv,
            device_id=who, device_id_type=MESH,
        )

    in_m = pltpu.make_async_copy(master, m_buf, in_sem.at[0])
    in_c = pltpu.make_async_copy(codes, x_buf.at[:, pl.ds(pl.multiple_of(q * 16, 16), 16)], in_sem.at[1])
    in_i = pltpu.make_async_copy(image.at[pl.ds(2 * pair, 2)], img_in, in_sem.at[2])
    in_mo = pltpu.make_async_copy(moment, mo_buf, in_sem.at[3])
    in_se = pltpu.make_async_copy(second, se_buf, in_sem.at[4])
    for copy in (in_m, in_c, in_i, in_mo, in_se):
        copy.start()

    barrier = pltpu.get_barrier_semaphore()
    for axis, size, me in (("row", ROWS, r), ("col", COLS, q), ("atom", ATOMS, t)):
        for d in range(1, size):
            pl.semaphore_signal(barrier, inc=1, device_id={axis: lax.rem(me + d, size)}, device_id_type=MESH)

    f_scr[...] = jnp.zeros_like(f_scr)
    in_m.wait()
    for i in range(4):
        for a in range(TAPS):
            f_scr[pl.ds((i * 8 + a) * 8, TAPS), :] = m_buf[i, a]
    for b in range(TAPS):
        f_buf[r, :, b * 128 : (b + 1) * 128] = f_scr[pl.ds(b, 32, stride=8), :].astype(BF16)

    pl.semaphore_wait(barrier, ROWS + COLS + ATOMS - 3)

    f_copies = []
    for d in range(1, ROWS):
        f_copies.append(
            remote(f_buf.at[r], f_buf.at[r], f_send.at[d - 1], f_recv.at[d - 1], {"row": lax.rem(r + d, ROWS)})
        )
        f_copies[-1].start()
    in_c.wait()
    own = x_buf.at[:, pl.ds(pl.multiple_of(q * 16, 16), 16)]
    c_copies = []
    for d in range(1, COLS):
        c_copies.append(remote(own, own, c_send.at[d - 1], c_recv.at[d - 1], {"col": lax.rem(q + d, COLS)}))
        c_copies[-1].start()

    in_i.wait()
    n = lax.broadcasted_iota(jnp.int32, (64, 128), 0)
    lane = lax.broadcasted_iota(jnp.int32, (64, 128), 1)
    band = (4 * half + ((n >> 2) & 3)) * 16 + (n >> 4) * 4 + (n & 3)
    pick = jnp.where(lane == band, 1.0, 0.0).astype(BF16)
    picked = lax.dot_general(
        pick, img_in[...].reshape(32, 128), (((1,), (1,)), ((), ())), preferred_element_type=F32
    ).astype(BF16)
    n = lax.broadcasted_iota(jnp.int32, (32, 128), 0)
    lane = lax.broadcasted_iota(jnp.int32, (32, 128), 1)
    place = jnp.where(lane == (n >> 4) * 64 + q * 16 + (n & 15), 1.0, 0.0).astype(BF16)
    img_out[...] = jnp.dot(picked, place, preferred_element_type=F32).astype(BF16).reshape(COLS, 16, 128)
    i_copies = []
    for d in range(1, COLS):
        to = lax.rem(q + d, COLS)
        i_copies.append(remote(img_out.at[to], img_got.at[d - 1], i_send.at[d - 1], i_recv.at[d - 1], {"col": to}))
        i_copies[-1].start()

    for copy in c_copies:
        copy.wait_recv()

    v = lax.broadcasted_iota(jnp.int32, (64, 128), 0)

    def shift_codes(u, carry):
        x = x_buf[u].astype(F32)
        for b in range(TAPS):
            s = b - 3
            moved = x if s == 0 else pltpu.roll(x, (-s) % 64, 0)
            if s:
                moved = jnp.where((v + s >= 0) & (v + s < 64), moved, 0.0)
            x7[pl.ds(pl.multiple_of(u * 64, 64), 64), b * 128 : (b + 1) * 128] = moved.astype(BF16)
        return carry

    lax.fori_loop(0, 16, shift_codes, 0)
    for copy in f_copies:
        copy.wait_recv()

    filters = f_buf[...].reshape(256, 896)
    product = lax.dot_general(filters, x7[...], (((1,), (1,)), ((), ())), preferred_element_type=F32)
    for j in range(8):
        pt[j] = product[:, j * 128 : (j + 1) * 128]

    lane = lax.broadcasted_iota(jnp.int32, (32, 128), 1)

    def swapped(x):
        return pltpu.roll(x, 64, 1)

    def tap(a, j):
        return pt[j, pl.ds(a, 32, stride=8), :]

    def add_taps(j, first):
        total = None
        for a in range(first, TAPS, 2):
            at = j - (6 + first - a) // 2
            if 0 <= at < 8:
                total = tap(a, at) if total is None else total + tap(a, at)
        return total if total is not None else jnp.zeros((32, 128), F32)

    evens = {}

    def even(j):
        if j not in evens:
            evens[j] = swapped(add_taps(j, 0)) if 0 <= j < 12 else jnp.zeros((32, 128), F32)
        return evens[j]

    def synth_tile(j):
        return add_taps(j, 1) + jnp.where(lane < 64, even(j - 1), even(j))

    above, below = lax.rem(r + ROWS - 1, ROWS), lax.rem(r + 1, ROWS)
    for at, j in enumerate((0, 1)):
        halo_out[0, at] = synth_tile(j).astype(BF16)
    to_above = remote(halo_out.at[0], halo_got.at[0], h_send.at[0], h_recv.at[0], {"row": above})
    to_above.start()
    for at, j in enumerate((10, 11)):
        halo_out[1, at] = synth_tile(j).astype(BF16)
    to_below = remote(halo_out.at[1], halo_got.at[1], h_send.at[1], h_recv.at[1], {"row": below})
    to_below.start()
    not_first = jnp.where(r > 0, 1.0, 0.0).astype(F32)
    not_last = jnp.where(r < ROWS - 1, 1.0, 0.0).astype(F32)
    mains = [synth_tile(2 + p) for p in range(8)]

    def put(p, value):
        part_out[2 * p] = value[:16].astype(BF16)
        part_out[2 * p + 1] = value[16:].astype(BF16)

    for p in range(2, 6):
        put(p, mains[p])
    to_above.wait_recv()
    for at in range(2):
        put(6 + at, mains[6 + at] + not_last * halo_got[0, at].astype(F32))
    to_below.wait_recv()
    for at in range(2):
        put(at, mains[at] + not_first * halo_got[1, at].astype(F32))
    p_copies = []
    for d in range(1, ATOMS):
        to = lax.rem(t + d, ATOMS)
        p_copies.append(remote(part_out.at[to], part_got.at[d - 1], p_send.at[d - 1], p_recv.at[d - 1], {"atom": to}))
        p_copies[-1].start()
    for copy in i_copies:
        copy.wait_recv()
    own_image = img_out[q].astype(F32)
    for d in range(COLS - 1):
        own_image = own_image + img_got[d].astype(F32)
    for copy in p_copies:
        copy.wait_recv()
    synth = part_out[t].astype(F32)
    for d in range(ATOMS - 1):
        synth = synth + part_got[d].astype(F32)
    resid[t] = (synth - own_image).astype(BF16)
    r_copies = []
    for d in range(1, ATOMS):
        to = lax.rem(t + d, ATOMS)
        r_copies.append(remote(resid.at[t], resid.at[t], r_send.at[d - 1], r_recv.at[d - 1], {"atom": to}))
        r_copies[-1].start()
    for copy in r_copies:
        copy.wait_recv()
    e_copies = [
        remote(resid.at[pl.ds(0, 4)], edge_got.at[1], e_send.at[0], e_recv.at[0], {"row": above}),
        remote(resid.at[pl.ds(12, 4)], edge_got.at[0], e_send.at[1], e_recv.at[1], {"row": below}),
    ]
    for copy in e_copies:
        copy.start()

    def tile_of(ref, p):
        return jnp.concatenate([ref[2 * p], ref[2 * p + 1]], axis=0).astype(F32)

    tiles = {2 + p: tile_of(resid, p) for p in range(8)}
    for copy in e_copies:
        copy.wait_recv()
    for at in range(2):
        tiles[at] = not_first * tile_of(edge_got.at[0], at)
        tiles[10 + at] = not_last * tile_of(edge_got.at[1], at)
    turned = {j: swapped(tiles[j]) for j in range(12)}
    between = {j: jnp.where(lane < 64, turned[j], turned[j + 1]) for j in range(11)}
    for a in range(8):
        for j in range(8):
            tile = tiles[j + (7 - a) // 2] if a % 2 else between[j + (6 - a) // 2]
            xr[j, pl.ds(a, 32, stride=8), :] = tile
    for j in range(8):
        xrb[:, j * 128 : (j + 1) * 128] = xr[j].astype(BF16)

    grad = jnp.dot(xrb[...], x7[...], preferred_element_type=F32)
    g_out[...] = grad.astype(BF16).reshape(ROWS, 32, 896)
    g_copies = []
    for d in range(1, ROWS):
        to = lax.rem(r + d, ROWS)
        g_copies.append(remote(g_out.at[to], g_got.at[d - 1], g_send.at[d - 1], g_recv.at[d - 1], {"row": to}))
        g_copies[-1].start()

    p2[...] = lax.dot_general(
        xrb[...], f_buf[...].reshape(256, 896), (((0,), (0,)), ((), ())), preferred_element_type=F32
    )

    def shift_back(u, carry):
        total = p2[pl.ds(pl.multiple_of(u * 64, 64), 64), 384:512]
        for b in range(TAPS):
            s = b - 3
            if s:
                x = p2[pl.ds(pl.multiple_of(u * 64, 64), 64), b * 128 : (b + 1) * 128]
                moved = pltpu.roll(x, s % 64, 0)
                total = total + jnp.where((v - s >= 0) & (v - s < 64), moved, 0.0)
        bk_out[u] = total.astype(BF16)
        return carry

    lax.fori_loop(0, 16, shift_back, 0)
    b_copies = []
    for d in range(1, COLS):
        to = lax.rem(q + d, COLS)
        b_copies.append(
            remote(
                bk_out.at[:, pl.ds(pl.multiple_of(to * 16, 16), 16)],
                bk_got.at[d - 1], b_send.at[d - 1], b_recv.at[d - 1], {"col": to},
            )
        )
        b_copies[-1].start()
    for copy in b_copies:
        copy.wait_recv()
    mine = pl.ds(pl.multiple_of(q * 16, 16), 16)

    def shrink(u, carry):
        back = bk_out[u, mine].astype(F32)
        for d in range(COLS - 1):
            back = back + bk_got[d, u].astype(F32)
        moved = x_buf[u, mine].astype(F32) - 0.05 * back
        out_codes[u] = (moved - jnp.clip(moved, -0.02, 0.02)).astype(BF16)
        return carry

    lax.fori_loop(0, 16, shrink, 0)

    in_mo.wait()
    in_se.wait()
    for copy in g_copies:
        copy.wait_recv()
    for b in range(TAPS):
        cols = slice(b * 128, (b + 1) * 128)
        total = g_out[r, :, cols].astype(F32)
        for d in range(ROWS - 1):
            total = total + g_got[d, :, cols].astype(F32)
        g_scr[pl.ds(b, 32, stride=8), :] = total
    for i in range(4):
        for a in range(TAPS):
            grad = g_scr[pl.ds((i * 8 + a) * 8, TAPS), :]
            new_moment = 0.9 * mo_buf[i, a] + 0.1 * grad
            new_second = 0.999 * se_buf[i, a] + 0.001 * grad * grad
            out_moment[i, a] = new_moment
            out_second[i, a] = new_second
            out_dict[i, a] = m_buf[i, a] - 0.05 * (new_moment / first_fix) / (
                jnp.sqrt(new_second / second_fix) + 1e-08
            )

    for copy in f_copies + c_copies + i_copies + [to_above, to_below] + p_copies + r_copies + e_copies + g_copies + b_copies:
        copy.wait_send()


def local(codes, image, master, moment, second):
    dma = pltpu.SemaphoreType.DMA
    vmem = pltpu.VMEM
    any_spec = pl.BlockSpec(memory_space=pl.ANY)
    vmem_spec = pl.BlockSpec(memory_space=vmem)
    return pl.pallas_call(
        kernel,
        out_shape=(
            jax.ShapeDtypeStruct(codes.shape, BF16),
            jax.ShapeDtypeStruct(master.shape, F32),
            jax.ShapeDtypeStruct(master.shape, F32),
            jax.ShapeDtypeStruct(master.shape, F32),
        ),
        in_specs=[any_spec] * 5,
        out_specs=(vmem_spec,) * 4,
        scratch_shapes=[
            vmem((16, 64, 128), BF16),
            vmem((1024, 896), BF16),
            vmem((8, 32, 896), BF16),
            vmem((256, 128), F32),
            vmem(master.shape, F32),
            vmem(master.shape, F32),
            vmem(master.shape, F32),
            vmem((2, 16, 128), BF16),
            vmem((4, 16, 128), BF16),
            vmem((3, 16, 128), BF16),
            vmem((8, 256, 128), F32),
            vmem((2, 2, 32, 128), BF16),
            vmem((2, 2, 32, 128), BF16),
            vmem((16, 16, 128), BF16),
            vmem((15, 16, 128), BF16),
            vmem((16, 16, 128), BF16),
            vmem((2, 4, 16, 128), BF16),
            vmem((8, 256, 128), F32),
            vmem((256, 1024), BF16),
            vmem((8, 32, 896), BF16),
            vmem((7, 32, 896), BF16),
            vmem((1024, 896), F32),
            vmem((16, 64, 128), BF16),
            vmem((3, 16, 16, 128), BF16),
            vmem((256, 128), F32),
            dma((5,)),
            dma((7,)), dma((7,)), dma((3,)), dma((3,)), dma((3,)), dma((3,)),
            dma((2,)), dma((2,)), dma((15,)), dma((15,)), dma((15,)), dma((15,)), dma((2,)), dma((2,)),
            dma((7,)), dma((7,)), dma((3,)), dma((3,)),
        ],
        compiler_params=pltpu.CompilerParams(
            collective_id=0, has_side_effects=True, vmem_limit_bytes=40 * 1024 * 1024
        ),
        name="dictionary_step",
    )(codes, image, master, moment, second)


def solution(mesh):
    tile = P("row", "col", "atom")
    bank = P(("row", "col"), None, None, "atom")
    return jax.shard_map(
        local,
        mesh=mesh,
        in_specs=(tile, P("row", "col", None), bank, bank, bank),
        out_specs=(tile, bank, bank, bank),
        check_vma=False,
    )
```

```python
import functools

import jax
import jax.numpy as jnp
from jax import lax
from jax.experimental import pallas as pl
from jax.experimental.pallas import tpu as pltpu
from jax.sharding import PartitionSpec as P

MESH = pl.DeviceIdType.MESH
F32, BF16 = jnp.float32, jnp.bfloat16
first_fix = 0.9999734386011124
second_fix = 0.09520785288629038
ROWS, COLS, ATOMS = 8, 4, 16
TAPS = 7


def kernel(
    codes, image, master,
    out_codes, out_grad,
    x_buf, x7, f_buf, m_buf,
    img_in, img_out, img_got,
    pt, part_out, part_got,
    resid, edge_got, xrg, xrb,
    g_out, g_sum, g_got, p2, bk_out, bk_sum, bk_got,
    in_sem, f_send, f_recv, c_send, c_recv, i_send, i_recv,
    z_send, z_recv, p_send, p_recv, r_send, r_recv, e_send, e_recv,
    g_send, g_recv, b_send, b_recv,
):
    r = lax.axis_index("row")
    q = lax.axis_index("col")
    t = lax.axis_index("atom")
    pair, half = t // 2, lax.rem(t, 2)
    started = []

    def start(copy):
        copy.start()
        started.append(copy)
        return copy

    def remote(src, dst, send, recv, who):
        return pltpu.make_async_remote_copy(
            src_ref=src, dst_ref=dst, send_sem=send, recv_sem=recv,
            device_id=who, device_id_type=MESH,
        )

    def row_at(d):
        return lax.rem(r + d + 2 * ROWS, ROWS)

    def col_at(d):
        return lax.rem(q + d + 2 * COLS, COLS)

    def tile_cols(at):
        return pl.ds(pl.multiple_of(at * 16, 16), 16)

    in_m = pltpu.make_async_copy(master, m_buf, in_sem.at[0])
    in_c = pltpu.make_async_copy(codes, x_buf.at[pl.ds(3, 16), tile_cols(q)], in_sem.at[1])
    in_i = pltpu.make_async_copy(image.at[pl.ds(2 * pair, 2)], img_in, in_sem.at[2])
    for copy in (in_m, in_c, in_i):
        copy.start()

    barrier = pltpu.get_barrier_semaphore()
    peers = [{"row": row_at(d)} for d in (1, -1, 2, -2)]
    peers += [{"col": col_at(d)} for d in range(1, COLS)]
    peers += [{"atom": lax.rem(t + d, ATOMS)} for d in range(1, ATOMS)]
    for who in peers:
        pl.semaphore_signal(barrier, inc=1, device_id=who, device_id_type=MESH)

    in_m.wait()
    for b in range(TAPS):
        rows = [m_buf[a * TAPS + b] for a in range(TAPS)] + [jnp.zeros((4, 128), F32)]
        f_buf[r, :, b * 128 : (b + 1) * 128] = jnp.concatenate(rows, axis=0).astype(BF16)

    pl.semaphore_wait(barrier, len(peers))

    def side(way):
        return 1 if way == 0 else -1

    @functools.cache
    def f_hop(way, kind):
        step, sem = side(way), way * 4 + kind
        rows = pl.ds(16 * way, 16) if kind == 3 else slice(None)
        piece = f_buf.at[r if kind < 2 else row_at(-2 * step), rows]
        to = row_at(step if kind in (0, 2) else 2 * step)
        return remote(piece, piece, f_send.at[sem], f_recv.at[sem], {"row": to})

    first = (3, 11, 0, 19)
    count = (8, 8, 3, 3)

    @functools.cache
    def c_hop(way, s, c):
        step = side(way)
        piece = x_buf.at[pl.ds(first[c], count[c]), tile_cols(col_at(-step * (s - 1)))]
        sem = (way * 2 + s - 1) * 4 + c
        return remote(piece, piece, c_send.at[sem], c_recv.at[sem], {"col": col_at(step)})

    @functools.cache
    def z_hop(way):
        step = side(way)
        src = x_buf.at[pl.ds(16 if way == 0 else 3, 3), tile_cols(q)]
        dst = x_buf.at[pl.ds(0 if way == 0 else 19, 3), tile_cols(q)]
        return remote(src, dst, z_send.at[way], z_recv.at[way], {"row": row_at(step)})

    def chunk(way, k):
        return k if way == 0 else 1 - k

    for way in range(2):
        start(f_hop(way, 1))
    in_c.wait()
    for way in range(2):
        start(z_hop(way))
    for way in range(2):
        start(f_hop(way, 0))
    for k in range(2):
        for way in range(2):
            start(c_hop(way, 1, chunk(way, k)))

    in_i.wait()
    n = lax.broadcasted_iota(jnp.int32, (64, 128), 0)
    lane = lax.broadcasted_iota(jnp.int32, (64, 128), 1)
    band = (4 * half + ((n >> 2) & 3)) * 16 + (n >> 4) * 4 + (n & 3)
    pick = jnp.where(lane == band, 1.0, 0.0).astype(BF16)
    picked = lax.dot_general(
        pick, img_in[...].reshape(32, 128), (((1,), (1,)), ((), ())), preferred_element_type=F32
    ).astype(BF16)
    n = lax.broadcasted_iota(jnp.int32, (32, 128), 0)
    lane = lax.broadcasted_iota(jnp.int32, (32, 128), 1)
    place = jnp.where(lane == (n >> 4) * 64 + q * 16 + (n & 15), 1.0, 0.0).astype(BF16)
    img_out[...] = jnp.dot(picked, place, preferred_element_type=F32).astype(BF16).reshape(COLS, 16, 128)

    for way in range(2):
        z_hop(way).wait_recv()
    for way in range(2):
        for k in range(2):
            start(c_hop(way, 1, 2 + chunk(way, k)))
    for way in range(2):
        f_hop(way, 1).wait_recv()
        start(f_hop(way, 2))
        start(f_hop(way, 3))
    for way in range(2):
        c_hop(way, 1, way).wait_recv()
        start(c_hop(way, 2, way))
    for way in range(2):
        c_hop(way, 1, 2 + way).wait_recv()
        start(c_hop(way, 2, 2 + way))
    i_copies = []
    for d in range(1, COLS):
        to = col_at(d)
        i_copies.append(
            start(remote(img_out.at[to], img_got.at[d - 1], i_send.at[d - 1], i_recv.at[d - 1], {"col": to}))
        )

    v = lax.broadcasted_iota(jnp.int32, (64, 128), 0)

    def shift_codes(e, carry):
        x = x_buf[e].astype(F32)
        inside = ((e >= 3) | (r > 0)) & ((e < 19) | (r < ROWS - 1))
        x = jnp.where(inside, x, 0.0)
        for b in range(TAPS):
            s = b - 3
            moved = x if s == 0 else pltpu.roll(x, (-s) % 64, 0)
            if s:
                moved = jnp.where((v + s >= 0) & (v + s < 64), moved, 0.0)
            x7[pl.ds(pl.multiple_of(e * 64, 64), 64), b * 128 : (b + 1) * 128] = moved.astype(BF16)
        return carry

    for way in range(2):
        c_hop(way, 1, 1 - way).wait_recv()
        c_hop(way, 1, 3 - way).wait_recv()
    c_hop(0, 2, 0).wait_recv()
    lax.fori_loop(3, 11, shift_codes, 0)
    c_hop(1, 2, 1).wait_recv()
    lax.fori_loop(11, 19, shift_codes, 0)
    c_hop(0, 2, 2).wait_recv()
    lax.fori_loop(0, 3, shift_codes, 0)
    c_hop(1, 2, 3).wait_recv()
    lax.fori_loop(19, 22, shift_codes, 0)
    for way in range(2):
        for kind in (0, 2, 3):
            f_hop(way, kind).wait_recv()

    product = lax.dot_general(
        f_buf[...].reshape(256, 896), x7[...], (((1,), (1,)), ((), ())), preferred_element_type=F32
    )
    pt[...] = product.reshape(8, 4, 8, 1408)

    lane = lax.broadcasted_iota(jnp.int32, (32, 128), 1)
    low = lax.broadcasted_iota(jnp.int32, (4, 8, 128), 1) < 4

    def swapped(x):
        return pltpu.roll(x, 64, 1)

    def turned(x):
        return pltpu.roll(x, 4, 1)

    def tap_sums(j):
        total = None
        for m in range(4):
            if j + m < 11:
                term = pt[:, m, :, (j + m) * 128 : (j + m + 1) * 128]
                total = term if total is None else total + term
        total = total.reshape(4, 2, 8, 128)
        one, two = total[:, 0], total[:, 1]
        even = jnp.where(low, one, turned(two)).reshape(32, 128)
        odd = jnp.where(low, turned(one), two).reshape(32, 128)
        return even, swapped(odd)

    even, odd = tap_sums(0)
    for p in range(8):
        next_even, next_odd = tap_sums(p + 1)
        value = even + jnp.where(lane < 64, odd, next_odd)
        part_out[2 * p] = value[:16].astype(BF16)
        part_out[2 * p + 1] = value[16:].astype(BF16)
        even, odd = next_even, next_odd
    p_copies = []
    for d in range(1, ATOMS):
        to = lax.rem(t + d, ATOMS)
        p_copies.append(
            start(remote(part_out.at[to], part_got.at[d - 1], p_send.at[d - 1], p_recv.at[d - 1], {"atom": to}))
        )
    for copy in i_copies:
        copy.wait_recv()
    own_image = img_out[q].astype(F32)
    for d in range(COLS - 1):
        own_image = own_image + img_got[d].astype(F32)
    synth = part_out[t].astype(F32)
    for copy in p_copies:
        copy.wait_recv()
    for d in range(ATOMS - 1):
        synth = synth + part_got[d].astype(F32)
    resid[t] = (synth - own_image).astype(BF16)
    r_copies = []
    for d in range(1, ATOMS):
        to = lax.rem(t + d, ATOMS)
        r_copies.append(
            start(remote(resid.at[t], resid.at[t], r_send.at[d - 1], r_recv.at[d - 1], {"atom": to}))
        )
    for copy in r_copies:
        copy.wait_recv()
    e_copies = [
        start(remote(resid.at[pl.ds(0, 4)], edge_got.at[1], e_send.at[0], e_recv.at[0], {"row": row_at(-1)})),
        start(remote(resid.at[pl.ds(12, 4)], edge_got.at[0], e_send.at[1], e_recv.at[1], {"row": row_at(1)})),
    ]

    def tile_of(ref, p):
        return jnp.concatenate([ref[2 * p], ref[2 * p + 1]], axis=0).astype(F32)

    tiles = {2 + p: tile_of(resid, p) for p in range(8)}
    flipped = {j: swapped(tiles[j]) for j in range(2, 10)}
    zero = jnp.zeros((32, 128), F32)

    def paired(even, odd):
        even, odd = even.reshape(4, 8, 128), odd.reshape(4, 8, 128)
        one, two = jnp.where(low, even, turned(odd)), jnp.where(low, turned(even), odd)
        return jnp.stack([one, two], axis=1).reshape(8, 8, 128)

    shares = [
        paired(tiles.get(j + 2, zero), jnp.where(lane < 64, flipped.get(j + 1, zero), flipped.get(j + 2, zero)))
        if j < 8 else paired(zero, jnp.where(lane < 64, flipped[9], zero))
        for j in range(9)
    ]
    none = jnp.zeros((8, 8, 128), F32)
    for j in range(11):
        taps = [shares[j - m] if 0 <= j - m < 9 else none for m in range(4)]
        xrg[:, j * 128 : (j + 1) * 128] = jnp.stack(taps, axis=1).reshape(256, 128).astype(BF16)

    grad = jnp.dot(xrg[...], x7[...], preferred_element_type=F32)
    g_out[...] = grad.astype(BF16).reshape(ROWS, 32, 896)

    @functools.cache
    def g_hop(way, kind):
        step, sem = side(way), way * 4 + kind
        rows = pl.ds(16 * way, 16) if kind == 1 else slice(None)
        src = g_sum.at[way] if kind == 3 else g_out.at[row_at(step * (3, 4, 1)[kind]), rows]
        to = row_at(step if kind in (0, 2) else 2 * step)
        return remote(src, g_got.at[way, kind, rows], g_send.at[sem], g_recv.at[sem], {"row": to})

    def g_relay():
        for way in range(2):
            g_hop(way, 0).wait_recv()
            g_hop(way, 1).wait_recv()
            dest = row_at(2 * side(way))
            term = g_out[dest].astype(F32) + g_got[way, 0].astype(F32)
            near = slice(16 * way, 16 * way + 16)
            far = slice(16 - 16 * way, 32 - 16 * way)
            g_sum[way, near, :] = (term[near] + g_got[way, 1, near, :].astype(F32)).astype(BF16)
            g_sum[way, far, :] = term[far].astype(BF16)
            start(g_hop(way, 3))

    for kind in range(3):
        for way in range(2):
            start(g_hop(way, kind))

    not_first = jnp.where(r > 0, 1.0, 0.0).astype(F32)
    not_last = jnp.where(r < ROWS - 1, 1.0, 0.0).astype(F32)
    for copy in e_copies:
        copy.wait_recv()
    for at in range(2):
        tiles[at] = not_first * tile_of(edge_got.at[0], at)
        tiles[10 + at] = not_last * tile_of(edge_got.at[1], at)
        flipped[at] = swapped(tiles[at])
        flipped[10 + at] = swapped(tiles[10 + at])
    both = [paired(jnp.where(lane < 64, flipped[j], flipped[j + 1]), tiles[j]) for j in range(11)]
    for j in range(8):
        tap_rows = jnp.stack([both[j + 3 - m] for m in range(4)], axis=1).reshape(256, 128)
        xrb[:, j * 128 : (j + 1) * 128] = tap_rows.astype(BF16)

    def back_part(at):
        cols = slice(at * 512, (at + 1) * 512)
        p2[...] = lax.dot_general(
            xrb[:, cols], f_buf[...].reshape(256, 896), (((0,), (0,)), ((), ())), preferred_element_type=F32
        )

        def shift_back(u, carry):
            here = pl.ds(pl.multiple_of(u * 64, 64), 64)
            total = p2[here, 384:512]
            for b in range(TAPS):
                s = b - 3
                if s:
                    moved = pltpu.roll(p2[here, b * 128 : (b + 1) * 128], s % 64, 0)
                    total = total + jnp.where((v - s >= 0) & (v - s < 64), moved, 0.0)
            bk_out[at * 8 + u] = total.astype(BF16)
            return carry

        lax.fori_loop(0, 8, shift_back, 0)

    @functools.cache
    def b_hop(way, s, c):
        step = side(way)
        rows = pl.ds(8 * c, 8)
        alone = s == 2 or c == chunk(way, 1)
        src = bk_out.at[rows, tile_cols(col_at(step * s))] if alone else bk_sum.at[way]
        sem = (way * 2 + s - 1) * 2 + c
        return remote(src, bk_got.at[way, s - 1, rows], b_send.at[sem], b_recv.at[sem], {"col": col_at(step)})

    def b_step(way):
        c = chunk(way, 0)
        b_hop(way, 2, c).wait_recv()
        own = bk_out[8 * c : 8 * c + 8, tile_cols(col_at(1 if way == 0 else -1)), :].astype(F32)
        bk_sum[way] = (own + bk_got[way, 1, 8 * c : 8 * c + 8].astype(F32)).astype(BF16)
        start(b_hop(way, 1, c))

    back_part(0)
    start(b_hop(0, 2, 0))
    start(b_hop(1, 1, 0))
    g_relay()
    back_part(1)
    start(b_hop(1, 2, 1))
    start(b_hop(0, 1, 1))
    b_step(0)
    b_step(1)
    for way in range(2):
        for c in range(2):
            b_hop(way, 1, c).wait_recv()

    def shrink(u, carry):
        back = bk_out[u, tile_cols(q)].astype(F32)
        for way in range(2):
            back = back + bk_got[way, 0, u].astype(F32)
        moved = x_buf[u + 3, tile_cols(q)].astype(F32) - 0.05 * back
        out_codes[u] = (moved - jnp.clip(moved, -0.02, 0.02)).astype(BF16)
        return carry

    lax.fori_loop(0, 16, shrink, 0)

    for way in range(2):
        for kind in (2, 3):
            g_hop(way, kind).wait_recv()
    for b in range(TAPS):
        cols = slice(b * 128, (b + 1) * 128)
        total = g_out[r, :, cols].astype(F32)
        for way in range(2):
            for kind in (2, 3):
                total = total + g_got[way, kind, :, cols].astype(F32)
        for a in range(TAPS):
            out_grad[a * TAPS + b] = total[4 * a : 4 * a + 4]

    for copy in started:
        copy.wait_send()


def adam_update(master, moment, second, grad):
    new_moment = 0.9 * moment + 0.1 * grad
    new_second = 0.999 * second + 0.001 * grad * grad
    new_dictionary = master - 0.05 * (new_moment / first_fix) / (
        jnp.sqrt(new_second / second_fix) + 1e-08
    )
    return (new_dictionary, new_moment, new_second)


def local(codes, image, master, moment, second):
    dma = pltpu.SemaphoreType.DMA
    vmem = pltpu.VMEM
    hbm_spec = pl.BlockSpec(memory_space=pltpu.HBM)
    vmem_spec = pl.BlockSpec(memory_space=vmem)
    bands = master.shape[0]
    taps = TAPS * TAPS
    new_codes, grad = pl.pallas_call(
        kernel,
        out_shape=(
            jax.ShapeDtypeStruct(codes.shape, BF16),
            jax.ShapeDtypeStruct((taps, bands, 128), F32),
        ),
        in_specs=[hbm_spec] * 3,
        out_specs=(vmem_spec,) * 2,
        scratch_shapes=[
            vmem((22, 64, 128), BF16),
            vmem((1408, 896), BF16),
            vmem((8, 32, 896), BF16),
            vmem((taps, bands, 128), F32),
            vmem((2, 16, 128), BF16),
            vmem((4, 16, 128), BF16),
            vmem((3, 16, 128), BF16),
            vmem((8, 4, 8, 1408), F32),
            vmem((16, 16, 128), BF16),
            vmem((15, 16, 128), BF16),
            vmem((16, 16, 128), BF16),
            vmem((2, 4, 16, 128), BF16),
            vmem((256, 1408), BF16),
            vmem((256, 1024), BF16),
            vmem((8, 32, 896), BF16),
            vmem((2, 32, 896), BF16),
            vmem((2, 4, 32, 896), BF16),
            vmem((512, 896), F32),
            vmem((16, 64, 128), BF16),
            vmem((2, 8, 16, 128), BF16),
            vmem((2, 2, 16, 16, 128), BF16),
            dma((3,)),
            dma((8,)), dma((8,)), dma((16,)), dma((16,)), dma((3,)), dma((3,)),
            dma((2,)), dma((2,)), dma((15,)), dma((15,)), dma((15,)), dma((15,)), dma((2,)), dma((2,)),
            dma((8,)), dma((8,)), dma((8,)), dma((8,)),
        ],
        compiler_params=pltpu.CompilerParams(
            collective_id=0, has_side_effects=True, vmem_limit_bytes=60 * 1024 * 1024
        ),
        name="dictionary_step",
    )(codes, image, jnp.transpose(master, (1, 2, 0, 3)).reshape(taps, bands, 128))
    grad = jnp.transpose(grad.reshape(TAPS, TAPS, bands, 128), (2, 0, 1, 3))
    return (new_codes, *adam_update(master, moment, second, grad))


def solution(mesh):
    tile = P("row", "col", "atom")
    bank = P(("row", "col"), None, None, "atom")
    return jax.shard_map(
        local,
        mesh=mesh,
        in_specs=(tile, P("row", "col", None), bank, bank, bank),
        out_specs=(tile, bank, bank, bank),
        check_vma=False,
    )
```

```python
import functools

import jax
import jax.numpy as jnp
from jax import lax
from jax.experimental import pallas as pl
from jax.experimental.pallas import tpu as pltpu
from jax.sharding import PartitionSpec as P

MESH = pl.DeviceIdType.MESH
F32, BF16 = jnp.float32, jnp.bfloat16
first_fix = 0.9999734386011124
second_fix = 0.09520785288629038
ROWS, COLS, ATOMS = 8, 4, 16
TAPS = 7


def kernel(
    codes, image, master,
    out_codes, out_grad,
    x_buf, x_edge, x7, f_buf, m_buf,
    img_in, img_out, img_got,
    pt, part_out, part_got,
    resid, edge_got, xrg, xrb,
    g_out, g_sum, g_got, p2, bk_out, bk_sum, bk_got,
    in_sem, f_send, f_recv, c_send, c_recv, i_send, i_recv,
    z_send, z_recv, h_send, h_recv, p_send, p_recv, r_send, r_recv, e_send, e_recv,
    g_send, g_recv, b_send, b_recv,
):
    r = lax.axis_index("row")
    q = lax.axis_index("col")
    t = lax.axis_index("atom")
    pair, half = t // 2, lax.rem(t, 2)
    started = []

    def start(copy):
        copy.start()
        started.append(copy)
        return copy

    def remote(src, dst, send, recv, who):
        return pltpu.make_async_remote_copy(
            src_ref=src, dst_ref=dst, send_sem=send, recv_sem=recv,
            device_id=who, device_id_type=MESH,
        )

    def row_at(d):
        return lax.rem(r + d + 2 * ROWS, ROWS)

    def col_at(d):
        return lax.rem(q + d + 2 * COLS, COLS)

    def tile_cols(at):
        return pl.ds(pl.multiple_of(at * 16, 16), 16)

    in_m = pltpu.make_async_copy(master, m_buf, in_sem.at[0])
    in_c = pltpu.make_async_copy(codes, x_buf.at[:, tile_cols(q)], in_sem.at[1])
    in_i = pltpu.make_async_copy(image.at[pl.ds(2 * pair, 2)], img_in, in_sem.at[2])
    for copy in (in_m, in_c, in_i):
        copy.start()

    barrier = pltpu.get_barrier_semaphore()
    peers = [{"row": row_at(d)} for d in (1, -1, 2, -2)]
    peers += [{"col": col_at(d)} for d in range(1, COLS)]
    peers += [{"atom": lax.rem(t + d, ATOMS)} for d in range(1, ATOMS)]
    for who in peers:
        pl.semaphore_signal(barrier, inc=1, device_id=who, device_id_type=MESH)

    in_m.wait()
    for b in range(TAPS):
        rows = [m_buf[a * TAPS + b] for a in range(TAPS)] + [jnp.zeros((4, 128), F32)]
        f_buf[r, :, b * 128 : (b + 1) * 128] = jnp.concatenate(rows, axis=0).astype(BF16)

    pl.semaphore_wait(barrier, len(peers))

    def side(way):
        return 1 if way == 0 else -1

    @functools.cache
    def f_hop(way, kind):
        step, sem = side(way), way * 4 + kind
        rows = pl.ds(16 * way, 16) if kind == 3 else slice(None)
        piece = f_buf.at[r if kind < 2 else row_at(-2 * step), rows]
        to = row_at(step if kind in (0, 2) else 2 * step)
        return remote(piece, piece, f_send.at[sem], f_recv.at[sem], {"row": to})

    @functools.cache
    def c_hop(way, s, c):
        step = side(way)
        piece = x_buf.at[pl.ds(8 * c, 8), tile_cols(col_at(-step * (s - 1)))]
        sem = (way * 2 + s - 1) * 2 + c
        return remote(piece, piece, c_send.at[sem], c_recv.at[sem], {"col": col_at(step)})

    @functools.cache
    def z_hop(way):
        src = x_buf.at[pl.ds(13 if way == 0 else 0, 3), tile_cols(q)]
        dst = x_edge.at[pl.ds(3 * way, 3), tile_cols(q)]
        return remote(src, dst, z_send.at[way], z_recv.at[way], {"row": row_at(side(way))})

    @functools.cache
    def h_hop(d):
        piece = x_edge.at[:, tile_cols(q)]
        return remote(piece, piece, h_send.at[d - 1], h_recv.at[d - 1], {"col": col_at(d)})

    def chunk(way, k):
        return k if way == 0 else 1 - k

    for way in range(2):
        start(f_hop(way, 1))
    in_c.wait()
    for way in range(2):
        start(z_hop(way))
    for way in range(2):
        start(f_hop(way, 0))
    for k in range(2):
        for way in range(2):
            start(c_hop(way, 1, chunk(way, k)))

    in_i.wait()
    n = lax.broadcasted_iota(jnp.int32, (64, 128), 0)
    lane = lax.broadcasted_iota(jnp.int32, (64, 128), 1)
    band = (4 * half + ((n >> 2) & 3)) * 16 + (n >> 4) * 4 + (n & 3)
    pick = jnp.where(lane == band, 1.0, 0.0).astype(BF16)
    picked = lax.dot_general(
        pick, img_in[...].reshape(32, 128), (((1,), (1,)), ((), ())), preferred_element_type=F32
    ).astype(BF16)
    n = lax.broadcasted_iota(jnp.int32, (32, 128), 0)
    lane = lax.broadcasted_iota(jnp.int32, (32, 128), 1)
    place = jnp.where(lane == (n >> 4) * 64 + q * 16 + (n & 15), 1.0, 0.0).astype(BF16)
    img_out[...] = jnp.dot(picked, place, preferred_element_type=F32).astype(BF16).reshape(COLS, 16, 128)

    for way in range(2):
        z_hop(way).wait_recv()
    for d in (1, 3, 2):
        start(h_hop(d))
    for way in range(2):
        f_hop(way, 1).wait_recv()
        start(f_hop(way, 2))
        start(f_hop(way, 3))
    for way in range(2):
        c_hop(way, 1, way).wait_recv()
        start(c_hop(way, 2, way))
    i_copies = []
    for d in range(1, COLS):
        to = col_at(d)
        i_copies.append(
            start(remote(img_out.at[to], img_got.at[d - 1], i_send.at[d - 1], i_recv.at[d - 1], {"col": to}))
        )

    v = lax.broadcasted_iota(jnp.int32, (64, 128), 0)

    def shift_codes(x, at):
        x = x.astype(F32)
        for b in range(TAPS):
            s = b - 3
            moved = x if s == 0 else pltpu.roll(x, (-s) % 64, 0)
            if s:
                moved = jnp.where((v + s >= 0) & (v + s < 64), moved, 0.0)
            x7[pl.ds(pl.multiple_of(at * 64, 64), 64), b * 128 : (b + 1) * 128] = moved.astype(BF16)

    def shift_tile(u, carry):
        shift_codes(x_buf[u], u + 3)
        return carry

    def shift_edge(e, carry):
        x = x_edge[e]
        inside = jnp.where(e < 3, r, ROWS - 1 - r) > 0
        shift_codes(jnp.where(inside, x, jnp.zeros_like(x)), jnp.where(e < 3, e, e + 16))
        return carry

    for d in range(1, COLS):
        h_hop(d).wait_recv()
    lax.fori_loop(0, 6, shift_edge, 0)
    for way in range(2):
        c_hop(way, 1, 1 - way).wait_recv()
    c_hop(0, 2, 0).wait_recv()
    lax.fori_loop(0, 8, shift_tile, 0)
    c_hop(1, 2, 1).wait_recv()
    lax.fori_loop(8, 16, shift_tile, 0)
    for way in range(2):
        for kind in (0, 2, 3):
            f_hop(way, kind).wait_recv()

    product = lax.dot_general(
        f_buf[...].reshape(256, 896), x7[...], (((1,), (1,)), ((), ())), preferred_element_type=F32
    )
    pt[...] = product.reshape(8, 4, 8, 1408)

    lane = lax.broadcasted_iota(jnp.int32, (32, 128), 1)
    low = lax.broadcasted_iota(jnp.int32, (4, 8, 128), 1) < 4

    def swapped(x):
        return pltpu.roll(x, 64, 1)

    def turned(x):
        return pltpu.roll(x, 4, 1)

    def tap_sums(j):
        total = None
        for m in range(4):
            if j + m < 11:
                term = pt[:, m, :, (j + m) * 128 : (j + m + 1) * 128]
                total = term if total is None else total + term
        total = total.reshape(4, 2, 8, 128)
        one, two = total[:, 0], total[:, 1]
        even = jnp.where(low, one, turned(two)).reshape(32, 128)
        odd = jnp.where(low, turned(one), two).reshape(32, 128)
        return even, swapped(odd)

    even, odd = tap_sums(0)
    for p in range(8):
        next_even, next_odd = tap_sums(p + 1)
        value = even + jnp.where(lane < 64, odd, next_odd)
        part_out[2 * p] = value[:16].astype(BF16)
        part_out[2 * p + 1] = value[16:].astype(BF16)
        even, odd = next_even, next_odd
    p_copies = []
    for d in range(1, ATOMS):
        to = lax.rem(t + d, ATOMS)
        p_copies.append(
            start(remote(part_out.at[to], part_got.at[d - 1], p_send.at[d - 1], p_recv.at[d - 1], {"atom": to}))
        )
    for copy in i_copies:
        copy.wait_recv()
    own_image = img_out[q].astype(F32)
    for d in range(COLS - 1):
        own_image = own_image + img_got[d].astype(F32)
    synth = part_out[t].astype(F32)
    for copy in p_copies:
        copy.wait_recv()
    for d in range(ATOMS - 1):
        synth = synth + part_got[d].astype(F32)
    resid[t] = (synth - own_image).astype(BF16)
    r_copies = []
    for d in range(1, ATOMS):
        to = lax.rem(t + d, ATOMS)
        r_copies.append(
            start(remote(resid.at[t], resid.at[t], r_send.at[d - 1], r_recv.at[d - 1], {"atom": to}))
        )
    for copy in r_copies:
        copy.wait_recv()
    e_copies = [
        start(remote(resid.at[pl.ds(0, 4)], edge_got.at[1], e_send.at[0], e_recv.at[0], {"row": row_at(-1)})),
        start(remote(resid.at[pl.ds(12, 4)], edge_got.at[0], e_send.at[1], e_recv.at[1], {"row": row_at(1)})),
    ]

    def tile_of(ref, p):
        return jnp.concatenate([ref[2 * p], ref[2 * p + 1]], axis=0).astype(F32)

    tiles = {2 + p: tile_of(resid, p) for p in range(8)}
    flipped = {j: swapped(tiles[j]) for j in range(2, 10)}
    zero = jnp.zeros((32, 128), F32)

    def paired(even, odd):
        even, odd = even.reshape(4, 8, 128), odd.reshape(4, 8, 128)
        one, two = jnp.where(low, even, turned(odd)), jnp.where(low, turned(even), odd)
        return jnp.stack([one, two], axis=1).reshape(8, 8, 128)

    shares = [
        paired(tiles.get(j + 2, zero), jnp.where(lane < 64, flipped.get(j + 1, zero), flipped.get(j + 2, zero)))
        if j < 8 else paired(zero, jnp.where(lane < 64, flipped[9], zero))
        for j in range(9)
    ]
    none = jnp.zeros((8, 8, 128), F32)
    for j in range(11):
        taps = [shares[j - m] if 0 <= j - m < 9 else none for m in range(4)]
        xrg[:, j * 128 : (j + 1) * 128] = jnp.stack(taps, axis=1).reshape(256, 128).astype(BF16)

    grad = jnp.dot(xrg[...], x7[...], preferred_element_type=F32)
    g_out[...] = grad.astype(BF16).reshape(ROWS, 32, 896)

    @functools.cache
    def g_hop(way, kind):
        step, sem = side(way), way * 4 + kind
        rows = pl.ds(16 * way, 16) if kind == 1 else slice(None)
        src = g_sum.at[way] if kind == 3 else g_out.at[row_at(step * (3, 4, 1)[kind]), rows]
        to = row_at(step if kind in (0, 2) else 2 * step)
        return remote(src, g_got.at[way, kind, rows], g_send.at[sem], g_recv.at[sem], {"row": to})

    def g_relay():
        for way in range(2):
            g_hop(way, 0).wait_recv()
            g_hop(way, 1).wait_recv()
            dest = row_at(2 * side(way))
            term = g_out[dest].astype(F32) + g_got[way, 0].astype(F32)
            near = slice(16 * way, 16 * way + 16)
            far = slice(16 - 16 * way, 32 - 16 * way)
            g_sum[way, near, :] = (term[near] + g_got[way, 1, near, :].astype(F32)).astype(BF16)
            g_sum[way, far, :] = term[far].astype(BF16)
            start(g_hop(way, 3))

    for kind in range(3):
        for way in range(2):
            start(g_hop(way, kind))

    both = {}

    def rows_of_taps(slot, j):
        for at in range(j, j + 4):
            if at not in both:
                both[at] = paired(jnp.where(lane < 64, flipped[at], flipped[at + 1]), tiles[at])
        tap_rows = jnp.stack([both[j + 3 - m] for m in range(4)], axis=1).reshape(256, 128)
        xrb[:, slot * 128 : (slot + 1) * 128] = tap_rows.astype(BF16)

    for slot in range(4):
        rows_of_taps(slot, slot + 2)

    def back_part(at):
        cols = slice(at * 512, (at + 1) * 512)
        p2[...] = lax.dot_general(
            xrb[:, cols], f_buf[...].reshape(256, 896), (((0,), (0,)), ((), ())), preferred_element_type=F32
        )

        def shift_back(u, carry):
            here = pl.ds(pl.multiple_of(u * 64, 64), 64)
            total = p2[here, 384:512]
            for b in range(TAPS):
                s = b - 3
                if s:
                    moved = pltpu.roll(p2[here, b * 128 : (b + 1) * 128], s % 64, 0)
                    total = total + jnp.where((v - s >= 0) & (v - s < 64), moved, 0.0)
            bk_out[at * 8 + u] = total.astype(BF16)
            return carry

        lax.fori_loop(0, 8, shift_back, 0)

    @functools.cache
    def b_hop(way, s, c):
        step = side(way)
        rows = pl.ds(8 * c, 8)
        alone = s == 2 or c == chunk(way, 1)
        src = bk_out.at[rows, tile_cols(col_at(step * s))] if alone else bk_sum.at[way]
        sem = (way * 2 + s - 1) * 2 + c
        return remote(src, bk_got.at[way, s - 1, rows], b_send.at[sem], b_recv.at[sem], {"col": col_at(step)})

    def b_step(way):
        c = chunk(way, 0)
        b_hop(way, 2, c).wait_recv()
        own = bk_out[8 * c : 8 * c + 8, tile_cols(col_at(1 if way == 0 else -1)), :].astype(F32)
        bk_sum[way] = (own + bk_got[way, 1, 8 * c : 8 * c + 8].astype(F32)).astype(BF16)
        start(b_hop(way, 1, c))

    back_part(0)
    start(b_hop(0, 2, 0))
    start(b_hop(1, 1, 0))
    not_first = jnp.where(r > 0, 1.0, 0.0).astype(F32)
    not_last = jnp.where(r < ROWS - 1, 1.0, 0.0).astype(F32)
    for copy in e_copies:
        copy.wait_recv()
    for at in range(2):
        tiles[at] = not_first * tile_of(edge_got.at[0], at)
        tiles[10 + at] = not_last * tile_of(edge_got.at[1], at)
        flipped[at] = swapped(tiles[at])
        flipped[10 + at] = swapped(tiles[10 + at])
    for slot, j in enumerate((0, 1, 6, 7)):
        rows_of_taps(4 + slot, j)
    back_part(1)
    start(b_hop(1, 2, 1))
    start(b_hop(0, 1, 1))
    g_relay()
    b_step(0)
    b_step(1)
    for way in range(2):
        for c in range(2):
            b_hop(way, 1, c).wait_recv()

    def shrink(at, carry):
        u = jnp.where(at < 8, at + 4, jnp.where(at < 12, at - 8, at))
        back = bk_out[at, tile_cols(q)].astype(F32)
        for way in range(2):
            back = back + bk_got[way, 0, at].astype(F32)
        moved = x_buf[u, tile_cols(q)].astype(F32) - 0.05 * back
        out_codes[u] = (moved - jnp.clip(moved, -0.02, 0.02)).astype(BF16)
        return carry

    lax.fori_loop(0, 16, shrink, 0)

    for way in range(2):
        for kind in (2, 3):
            g_hop(way, kind).wait_recv()
    for b in range(TAPS):
        cols = slice(b * 128, (b + 1) * 128)
        total = g_out[r, :, cols].astype(F32)
        for way in range(2):
            for kind in (2, 3):
                total = total + g_got[way, kind, :, cols].astype(F32)
        for a in range(TAPS):
            out_grad[a * TAPS + b] = total[4 * a : 4 * a + 4]

    for copy in started:
        copy.wait_send()


def adam_update(master, moment, second, grad):
    new_moment = 0.9 * moment + 0.1 * grad
    new_second = 0.999 * second + 0.001 * grad * grad
    new_dictionary = master - 0.05 * (new_moment / first_fix) / (
        jnp.sqrt(new_second / second_fix) + 1e-08
    )
    return (new_dictionary, new_moment, new_second)


def local(codes, image, master, moment, second):
    dma = pltpu.SemaphoreType.DMA
    vmem = pltpu.VMEM
    hbm_spec = pl.BlockSpec(memory_space=pltpu.HBM)
    vmem_spec = pl.BlockSpec(memory_space=vmem)
    bands = master.shape[0]
    taps = TAPS * TAPS
    new_codes, grad = pl.pallas_call(
        kernel,
        out_shape=(
            jax.ShapeDtypeStruct(codes.shape, BF16),
            jax.ShapeDtypeStruct((taps, bands, 128), F32),
        ),
        in_specs=[hbm_spec] * 3,
        out_specs=(vmem_spec,) * 2,
        scratch_shapes=[
            vmem((16, 64, 128), BF16),
            vmem((6, 64, 128), BF16),
            vmem((1408, 896), BF16),
            vmem((8, 32, 896), BF16),
            vmem((taps, bands, 128), F32),
            vmem((2, 16, 128), BF16),
            vmem((4, 16, 128), BF16),
            vmem((3, 16, 128), BF16),
            vmem((8, 4, 8, 1408), F32),
            vmem((16, 16, 128), BF16),
            vmem((15, 16, 128), BF16),
            vmem((16, 16, 128), BF16),
            vmem((2, 4, 16, 128), BF16),
            vmem((256, 1408), BF16),
            vmem((256, 1024), BF16),
            vmem((8, 32, 896), BF16),
            vmem((2, 32, 896), BF16),
            vmem((2, 4, 32, 896), BF16),
            vmem((512, 896), F32),
            vmem((16, 64, 128), BF16),
            vmem((2, 8, 16, 128), BF16),
            vmem((2, 2, 16, 16, 128), BF16),
            dma((3,)),
            dma((8,)), dma((8,)), dma((8,)), dma((8,)), dma((3,)), dma((3,)),
            dma((2,)), dma((2,)), dma((3,)), dma((3,)), dma((15,)), dma((15,)), dma((15,)), dma((15,)), dma((2,)), dma((2,)),
            dma((8,)), dma((8,)), dma((8,)), dma((8,)),
        ],
        compiler_params=pltpu.CompilerParams(
            collective_id=0, has_side_effects=True, vmem_limit_bytes=60 * 1024 * 1024
        ),
        name="dictionary_step",
    )(codes, image, jnp.transpose(master, (1, 2, 0, 3)).reshape(taps, bands, 128))
    grad = jnp.transpose(grad.reshape(TAPS, TAPS, bands, 128), (2, 0, 1, 3))
    return (new_codes, *adam_update(master, moment, second, grad))


def solution(mesh):
    tile = P("row", "col", "atom")
    bank = P(("row", "col"), None, None, "atom")
    return jax.shard_map(
        local,
        mesh=mesh,
        in_specs=(tile, P("row", "col", None), bank, bank, bank),
        out_specs=(tile, bank, bank, bank),
        check_vma=False,
    )
```

```python
import functools

import jax
import jax.numpy as jnp
from jax import lax
from jax.experimental import pallas as pl
from jax.experimental.pallas import tpu as pltpu
from jax.sharding import PartitionSpec as P

MESH = pl.DeviceIdType.MESH
F32, BF16 = jnp.float32, jnp.bfloat16
first_fix = 0.9999734386011124
second_fix = 0.09520785288629038
ROWS, COLS, ATOMS = 8, 4, 16
TAPS = 7


def kernel(
    codes, image, master,
    out_codes, out_grad,
    x_buf, x_edge, x7, f_buf, m_buf,
    img_in, img_out, img_got,
    pt, part_out, part_got,
    resid, edge_got, xrg, xrb,
    g_out, g_sum, g_got, p2, bk_out, bk_sum, bk_got,
    in_sem, f_send, f_recv, c_send, c_recv, i_send, i_recv,
    z_send, z_recv, h_send, h_recv, p_send, p_recv, r_send, r_recv, e_send, e_recv,
    g_send, g_recv, b_send, b_recv,
):
    r = lax.axis_index("row")
    q = lax.axis_index("col")
    t = lax.axis_index("atom")
    pair, half = t // 2, lax.rem(t, 2)
    started = []

    def start(copy):
        copy.start()
        started.append(copy)
        return copy

    def remote(src, dst, send, recv, who):
        return pltpu.make_async_remote_copy(
            src_ref=src, dst_ref=dst, send_sem=send, recv_sem=recv,
            device_id=who, device_id_type=MESH,
        )

    def row_at(d):
        return lax.rem(r + d + 2 * ROWS, ROWS)

    def col_at(d):
        return lax.rem(q + d + 2 * COLS, COLS)

    def tile_cols(at):
        return pl.ds(pl.multiple_of(at * 16, 16), 16)

    in_m = pltpu.make_async_copy(master, m_buf, in_sem.at[0])
    in_c = pltpu.make_async_copy(codes, x_buf.at[:, tile_cols(q)], in_sem.at[1])
    in_i = pltpu.make_async_copy(image.at[pl.ds(2 * pair, 2)], img_in, in_sem.at[2])
    for copy in (in_m, in_c, in_i):
        copy.start()

    barrier = pltpu.get_barrier_semaphore()
    peers = [{"row": row_at(d)} for d in (1, -1, 2, -2)]
    peers += [{"col": col_at(d)} for d in range(1, COLS)]
    peers += [{"atom": lax.rem(t + d, ATOMS)} for d in range(1, ATOMS)]
    for who in peers:
        pl.semaphore_signal(barrier, inc=1, device_id=who, device_id_type=MESH)

    in_m.wait()
    for b in range(TAPS):
        rows = [m_buf[a * TAPS + b] for a in range(TAPS)] + [jnp.zeros((4, 128), F32)]
        f_buf[r, :, b * 128 : (b + 1) * 128] = jnp.concatenate(rows, axis=0).astype(BF16)

    pl.semaphore_wait(barrier, len(peers))

    def side(way):
        return 1 if way == 0 else -1

    @functools.cache
    def f_hop(way, kind):
        step, sem = side(way), way * 4 + kind
        rows = pl.ds(16 * way, 16) if kind == 3 else slice(None)
        piece = f_buf.at[r if kind < 2 else row_at(-2 * step), rows]
        to = row_at(step if kind in (0, 2) else 2 * step)
        return remote(piece, piece, f_send.at[sem], f_recv.at[sem], {"row": to})

    @functools.cache
    def c_hop(way, s, c):
        step = side(way)
        piece = x_buf.at[pl.ds(8 * c, 8), tile_cols(col_at(-step * (s - 1)))]
        sem = (way * 2 + s - 1) * 2 + c
        return remote(piece, piece, c_send.at[sem], c_recv.at[sem], {"col": col_at(step)})

    @functools.cache
    def z_hop(way):
        src = x_buf.at[pl.ds(13 if way == 0 else 0, 3), tile_cols(q)]
        dst = x_edge.at[pl.ds(3 * way, 3), tile_cols(q)]
        return remote(src, dst, z_send.at[way], z_recv.at[way], {"row": row_at(side(way))})

    @functools.cache
    def h_hop(d):
        piece = x_edge.at[:, tile_cols(q)]
        return remote(piece, piece, h_send.at[d - 1], h_recv.at[d - 1], {"col": col_at(d)})

    def chunk(way, k):
        return k if way == 0 else 1 - k

    in_c.wait()
    for way in range(2):
        start(c_hop(way, 1, way))
        start(f_hop(way, 1))
    for way in range(2):
        start(z_hop(way))
    for way in range(2):
        start(c_hop(way, 1, 1 - way))

    in_i.wait()
    n = lax.broadcasted_iota(jnp.int32, (64, 128), 0)
    lane = lax.broadcasted_iota(jnp.int32, (64, 128), 1)
    band = (4 * half + ((n >> 2) & 3)) * 16 + (n >> 4) * 4 + (n & 3)
    pick = jnp.where(lane == band, 1.0, 0.0).astype(BF16)
    picked = lax.dot_general(
        pick, img_in[...].reshape(32, 128), (((1,), (1,)), ((), ())), preferred_element_type=F32
    ).astype(BF16)
    n = lax.broadcasted_iota(jnp.int32, (32, 128), 0)
    lane = lax.broadcasted_iota(jnp.int32, (32, 128), 1)
    place = jnp.where(lane == (n >> 4) * 64 + q * 16 + (n & 15), 1.0, 0.0).astype(BF16)
    img_out[...] = jnp.dot(picked, place, preferred_element_type=F32).astype(BF16).reshape(COLS, 16, 128)

    for way in range(2):
        z_hop(way).wait_recv()
    for d in (1, 3, 2):
        start(h_hop(d))
    for way in range(2):
        c_hop(way, 1, way).wait_recv()
        start(c_hop(way, 2, way))
    for way in range(2):
        f_hop(way, 1).wait_recv()
        start(f_hop(way, 3))
        start(f_hop(way, 2))
    for way in range(2):
        start(f_hop(way, 0))
    v = lax.broadcasted_iota(jnp.int32, (64, 128), 0)

    def shift_codes(x, at):
        x = x.astype(F32)
        for b in range(TAPS):
            s = b - 3
            moved = x if s == 0 else pltpu.roll(x, (-s) % 64, 0)
            if s:
                moved = jnp.where((v + s >= 0) & (v + s < 64), moved, 0.0)
            x7[pl.ds(pl.multiple_of(at * 64, 64), 64), b * 128 : (b + 1) * 128] = moved.astype(BF16)

    def shift_tile(u, carry):
        shift_codes(x_buf[u], u + 3)
        return carry

    def shift_edge(e, carry):
        x = x_edge[e]
        inside = jnp.where(e < 3, r, ROWS - 1 - r) > 0
        shift_codes(jnp.where(inside, x, jnp.zeros_like(x)), jnp.where(e < 3, e, e + 16))
        return carry

    for d in range(1, COLS):
        h_hop(d).wait_recv()
    lax.fori_loop(0, 6, shift_edge, 0)
    for way in range(2):
        c_hop(way, 1, 1 - way).wait_recv()
    c_hop(0, 2, 0).wait_recv()
    lax.fori_loop(0, 8, shift_tile, 0)
    c_hop(1, 2, 1).wait_recv()
    lax.fori_loop(8, 16, shift_tile, 0)
    for way in range(2):
        for kind in (0, 2, 3):
            f_hop(way, kind).wait_recv()

    i_copies = []
    for d in range(1, COLS):
        to = col_at(d)
        i_copies.append(
            start(remote(img_out.at[to], img_got.at[d - 1], i_send.at[d - 1], i_recv.at[d - 1], {"col": to}))
        )

    product = lax.dot_general(
        f_buf[...].reshape(256, 896), x7[...], (((1,), (1,)), ((), ())), preferred_element_type=F32
    )
    pt[...] = product.reshape(8, 4, 8, 1408)

    lane = lax.broadcasted_iota(jnp.int32, (32, 128), 1)
    low = lax.broadcasted_iota(jnp.int32, (4, 8, 128), 1) < 4

    def swapped(x):
        return pltpu.roll(x, 64, 1)

    def turned(x):
        return pltpu.roll(x, 4, 1)

    def tap_sums(j):
        total = None
        for m in range(4):
            if j + m < 11:
                term = pt[:, m, :, (j + m) * 128 : (j + m + 1) * 128]
                total = term if total is None else total + term
        total = total.reshape(4, 2, 8, 128)
        one, two = total[:, 0], total[:, 1]
        even = jnp.where(low, one, turned(two)).reshape(32, 128)
        odd = jnp.where(low, turned(one), two).reshape(32, 128)
        return even, swapped(odd)

    even, odd = tap_sums(0)
    for p in range(8):
        next_even, next_odd = tap_sums(p + 1)
        value = even + jnp.where(lane < 64, odd, next_odd)
        part_out[2 * p] = value[:16].astype(BF16)
        part_out[2 * p + 1] = value[16:].astype(BF16)
        even, odd = next_even, next_odd
    p_copies = []
    for d in range(1, ATOMS):
        to = lax.rem(t + d, ATOMS)
        p_copies.append(
            start(remote(part_out.at[to], part_got.at[d - 1], p_send.at[d - 1], p_recv.at[d - 1], {"atom": to}))
        )
    for copy in i_copies:
        copy.wait_recv()
    own_image = img_out[q].astype(F32)
    for d in range(COLS - 1):
        own_image = own_image + img_got[d].astype(F32)
    synth = part_out[t].astype(F32)
    for copy in p_copies:
        copy.wait_recv()
    for d in range(ATOMS - 1):
        synth = synth + part_got[d].astype(F32)
    resid[t] = (synth - own_image).astype(BF16)
    r_copies = []
    for d in range(1, ATOMS):
        to = lax.rem(t + d, ATOMS)
        r_copies.append(
            start(remote(resid.at[t], resid.at[t], r_send.at[d - 1], r_recv.at[d - 1], {"atom": to}))
        )
    for copy in r_copies:
        copy.wait_recv()
    e_copies = [
        start(remote(resid.at[pl.ds(0, 4)], edge_got.at[1], e_send.at[0], e_recv.at[0], {"row": row_at(-1)})),
        start(remote(resid.at[pl.ds(12, 4)], edge_got.at[0], e_send.at[1], e_recv.at[1], {"row": row_at(1)})),
    ]

    def tile_of(ref, p):
        return jnp.concatenate([ref[2 * p], ref[2 * p + 1]], axis=0).astype(F32)

    tiles = {2 + p: tile_of(resid, p) for p in range(8)}
    flipped = {j: swapped(tiles[j]) for j in range(2, 10)}
    zero = jnp.zeros((32, 128), F32)

    def paired(even, odd):
        even, odd = even.reshape(4, 8, 128), odd.reshape(4, 8, 128)
        one, two = jnp.where(low, even, turned(odd)), jnp.where(low, turned(even), odd)
        return jnp.stack([one, two], axis=1).reshape(8, 8, 128)

    shares = [
        paired(tiles.get(j + 2, zero), jnp.where(lane < 64, flipped.get(j + 1, zero), flipped.get(j + 2, zero)))
        if j < 8 else paired(zero, jnp.where(lane < 64, flipped[9], zero))
        for j in range(9)
    ]
    none = jnp.zeros((8, 8, 128), F32)
    for j in range(11):
        taps = [shares[j - m] if 0 <= j - m < 9 else none for m in range(4)]
        xrg[:, j * 128 : (j + 1) * 128] = jnp.stack(taps, axis=1).reshape(256, 128).astype(BF16)

    grad = jnp.dot(xrg[...], x7[...], preferred_element_type=F32)
    g_out[...] = grad.astype(BF16).reshape(ROWS, 32, 896)

    @functools.cache
    def g_hop(way, kind):
        step, sem = side(way), way * 4 + kind
        rows = pl.ds(16 * way, 16) if kind == 1 else slice(None)
        src = g_sum.at[way] if kind == 3 else g_out.at[row_at(step * (3, 4, 1)[kind]), rows]
        to = row_at(step if kind in (0, 2) else 2 * step)
        return remote(src, g_got.at[way, kind, rows], g_send.at[sem], g_recv.at[sem], {"row": to})

    def g_relay():
        for way in range(2):
            g_hop(way, 0).wait_recv()
            g_hop(way, 1).wait_recv()
            dest = row_at(2 * side(way))
            term = g_out[dest].astype(F32) + g_got[way, 0].astype(F32)
            near = slice(16 * way, 16 * way + 16)
            far = slice(16 - 16 * way, 32 - 16 * way)
            g_sum[way, near, :] = (term[near] + g_got[way, 1, near, :].astype(F32)).astype(BF16)
            g_sum[way, far, :] = term[far].astype(BF16)
            start(g_hop(way, 3))

    for kind in range(2):
        for way in range(2):
            start(g_hop(way, kind))

    both = {}

    def rows_of_taps(slot, j):
        for at in range(j, j + 4):
            if at not in both:
                both[at] = paired(jnp.where(lane < 64, flipped[at], flipped[at + 1]), tiles[at])
        tap_rows = jnp.stack([both[j + 3 - m] for m in range(4)], axis=1).reshape(256, 128)
        xrb[:, slot * 128 : (slot + 1) * 128] = tap_rows.astype(BF16)

    for slot in range(4):
        rows_of_taps(slot, slot + 2)

    def back_part(at):
        cols = slice(at * 512, (at + 1) * 512)
        p2[...] = lax.dot_general(
            xrb[:, cols], f_buf[...].reshape(256, 896), (((0,), (0,)), ((), ())), preferred_element_type=F32
        )

        def shift_back(u, carry):
            here = pl.ds(pl.multiple_of(u * 64, 64), 64)
            total = p2[here, 384:512]
            for b in range(TAPS):
                s = b - 3
                if s:
                    moved = pltpu.roll(p2[here, b * 128 : (b + 1) * 128], s % 64, 0)
                    total = total + jnp.where((v - s >= 0) & (v - s < 64), moved, 0.0)
            bk_out[at * 8 + u] = total.astype(BF16)
            return carry

        lax.fori_loop(0, 8, shift_back, 0)

    @functools.cache
    def b_hop(way, s, c):
        step = side(way)
        rows = pl.ds(8 * c, 8)
        alone = s == 2 or c == chunk(way, 1)
        src = bk_out.at[rows, tile_cols(col_at(step * s))] if alone else bk_sum.at[way]
        sem = (way * 2 + s - 1) * 2 + c
        return remote(src, bk_got.at[way, s - 1, rows], b_send.at[sem], b_recv.at[sem], {"col": col_at(step)})

    def b_step(way):
        c = chunk(way, 0)
        b_hop(way, 2, c).wait_recv()
        own = bk_out[8 * c : 8 * c + 8, tile_cols(col_at(1 if way == 0 else -1)), :].astype(F32)
        bk_sum[way] = (own + bk_got[way, 1, 8 * c : 8 * c + 8].astype(F32)).astype(BF16)
        start(b_hop(way, 1, c))

    back_part(0)
    start(b_hop(0, 2, 0))
    start(b_hop(1, 1, 0))
    not_first = jnp.where(r > 0, 1.0, 0.0).astype(F32)
    not_last = jnp.where(r < ROWS - 1, 1.0, 0.0).astype(F32)
    for copy in e_copies:
        copy.wait_recv()
    for at in range(2):
        tiles[at] = not_first * tile_of(edge_got.at[0], at)
        tiles[10 + at] = not_last * tile_of(edge_got.at[1], at)
        flipped[at] = swapped(tiles[at])
        flipped[10 + at] = swapped(tiles[10 + at])
    for slot, j in enumerate((0, 1, 6, 7)):
        rows_of_taps(4 + slot, j)
    back_part(1)
    start(b_hop(1, 2, 1))
    start(b_hop(0, 1, 1))
    g_relay()
    for way in range(2):
        start(g_hop(way, 2))
    b_step(0)
    b_step(1)
    for way in range(2):
        for c in range(2):
            b_hop(way, 1, c).wait_recv()

    def shrink(at, carry):
        u = jnp.where(at < 8, at + 4, jnp.where(at < 12, at - 8, at))
        back = bk_out[at, tile_cols(q)].astype(F32)
        for way in range(2):
            back = back + bk_got[way, 0, at].astype(F32)
        moved = x_buf[u, tile_cols(q)].astype(F32) - 0.05 * back
        out_codes[u] = (moved - jnp.clip(moved, -0.02, 0.02)).astype(BF16)
        return carry

    lax.fori_loop(0, 16, shrink, 0)

    for way in range(2):
        for kind in (2, 3):
            g_hop(way, kind).wait_recv()
    for b in range(TAPS):
        cols = slice(b * 128, (b + 1) * 128)
        total = g_out[r, :, cols].astype(F32)
        for way in range(2):
            for kind in (2, 3):
                total = total + g_got[way, kind, :, cols].astype(F32)
        for a in range(TAPS):
            out_grad[a * TAPS + b] = total[4 * a : 4 * a + 4]

    for copy in started:
        copy.wait_send()


def adam_update(master, moment, second, grad):
    new_moment = 0.9 * moment + 0.1 * grad
    new_second = 0.999 * second + 0.001 * grad * grad
    new_dictionary = master - 0.05 * (new_moment / first_fix) / (
        jnp.sqrt(new_second / second_fix) + 1e-08
    )
    return (new_dictionary, new_moment, new_second)


def local(codes, image, master, moment, second):
    dma = pltpu.SemaphoreType.DMA
    vmem = pltpu.VMEM
    hbm_spec = pl.BlockSpec(memory_space=pltpu.HBM)
    vmem_spec = pl.BlockSpec(memory_space=vmem)
    bands = master.shape[0]
    taps = TAPS * TAPS
    new_codes, grad = pl.pallas_call(
        kernel,
        out_shape=(
            jax.ShapeDtypeStruct(codes.shape, BF16),
            jax.ShapeDtypeStruct((taps, bands, 128), F32),
        ),
        in_specs=[hbm_spec] * 3,
        out_specs=(vmem_spec,) * 2,
        scratch_shapes=[
            vmem((16, 64, 128), BF16),
            vmem((6, 64, 128), BF16),
            vmem((1408, 896), BF16),
            vmem((8, 32, 896), BF16),
            vmem((taps, bands, 128), F32),
            vmem((2, 16, 128), BF16),
            vmem((4, 16, 128), BF16),
            vmem((3, 16, 128), BF16),
            vmem((8, 4, 8, 1408), F32),
            vmem((16, 16, 128), BF16),
            vmem((15, 16, 128), BF16),
            vmem((16, 16, 128), BF16),
            vmem((2, 4, 16, 128), BF16),
            vmem((256, 1408), BF16),
            vmem((256, 1024), BF16),
            vmem((8, 32, 896), BF16),
            vmem((2, 32, 896), BF16),
            vmem((2, 4, 32, 896), BF16),
            vmem((512, 896), F32),
            vmem((16, 64, 128), BF16),
            vmem((2, 8, 16, 128), BF16),
            vmem((2, 2, 16, 16, 128), BF16),
            dma((3,)),
            dma((8,)), dma((8,)), dma((8,)), dma((8,)), dma((3,)), dma((3,)),
            dma((2,)), dma((2,)), dma((3,)), dma((3,)), dma((15,)), dma((15,)), dma((15,)), dma((15,)), dma((2,)), dma((2,)),
            dma((8,)), dma((8,)), dma((8,)), dma((8,)),
        ],
        compiler_params=pltpu.CompilerParams(
            collective_id=0, has_side_effects=True, vmem_limit_bytes=60 * 1024 * 1024
        ),
        name="dictionary_step",
    )(codes, image, jnp.transpose(master, (1, 2, 0, 3)).reshape(taps, bands, 128))
    grad = jnp.transpose(grad.reshape(TAPS, TAPS, bands, 128), (2, 0, 1, 3))
    return (new_codes, *adam_update(master, moment, second, grad))


def solution(mesh):
    tile = P("row", "col", "atom")
    bank = P(("row", "col"), None, None, "atom")
    return jax.shard_map(
        local,
        mesh=mesh,
        in_specs=(tile, P("row", "col", None), bank, bank, bank),
        out_specs=(tile, bank, bank, bank),
        check_vma=False,
    )
```

```python
import functools

import jax
import jax.numpy as jnp
from jax import lax
from jax.experimental import pallas as pl
from jax.experimental.pallas import tpu as pltpu
from jax.sharding import PartitionSpec as P

MESH = pl.DeviceIdType.MESH
F32, BF16 = jnp.float32, jnp.bfloat16
first_fix = 0.9999734386011124
second_fix = 0.09520785288629038
ROWS, COLS, ATOMS = 8, 4, 16
TAPS = 7


def kernel(
    codes, image, master,
    out_codes, out_grad,
    x_buf, x_edge, x7, f_buf, m_buf,
    img_in, img_out, img_got,
    pt, part_out, part_got,
    resid, edge_got, xrg, xrb,
    g_out, g_sum, g_got, p2, bk_out, bk_sum, bk_got,
    in_sem, f_send, f_recv, c_send, c_recv, i_send, i_recv,
    z_send, z_recv, h_send, h_recv, p_send, p_recv, r_send, r_recv, e_send, e_recv,
    g_send, g_recv, b_send, b_recv,
):
    r = lax.axis_index("row")
    q = lax.axis_index("col")
    t = lax.axis_index("atom")
    pair, half = t // 2, lax.rem(t, 2)
    started = []

    def start(copy):
        copy.start()
        started.append(copy)
        return copy

    def remote(src, dst, send, recv, who):
        return pltpu.make_async_remote_copy(
            src_ref=src, dst_ref=dst, send_sem=send, recv_sem=recv,
            device_id=who, device_id_type=MESH,
        )

    def row_at(d):
        return lax.rem(r + d + 2 * ROWS, ROWS)

    def col_at(d):
        return lax.rem(q + d + 2 * COLS, COLS)

    def tile_cols(at):
        return pl.ds(pl.multiple_of(at * 16, 16), 16)

    in_m = pltpu.make_async_copy(master, m_buf, in_sem.at[0])
    in_c = pltpu.make_async_copy(codes, x_buf.at[:, tile_cols(q)], in_sem.at[1])
    in_i = pltpu.make_async_copy(image.at[pl.ds(2 * pair, 2)], img_in, in_sem.at[2])
    for copy in (in_m, in_c, in_i):
        copy.start()

    barrier = pltpu.get_barrier_semaphore()
    peers = [{"row": row_at(d)} for d in (1, -1, 2, -2)]
    peers += [{"col": col_at(d)} for d in range(1, COLS)]
    peers += [{"atom": lax.rem(t + d, ATOMS)} for d in range(1, ATOMS)]
    for who in peers:
        pl.semaphore_signal(barrier, inc=1, device_id=who, device_id_type=MESH)

    in_m.wait()
    for b in range(TAPS):
        rows = [m_buf[a * TAPS + b] for a in range(TAPS)] + [jnp.zeros((4, 128), F32)]
        f_buf[r, :, b * 128 : (b + 1) * 128] = jnp.concatenate(rows, axis=0).astype(BF16)

    pl.semaphore_wait(barrier, len(peers))

    def side(way):
        return 1 if way == 0 else -1

    @functools.cache
    def f_hop(way, kind):
        step, sem = side(way), way * 4 + kind
        rows = pl.ds(16 * way, 16) if kind == 3 else slice(None)
        piece = f_buf.at[r if kind < 2 else row_at(-2 * step), rows]
        to = row_at(step if kind in (0, 2) else 2 * step)
        return remote(piece, piece, f_send.at[sem], f_recv.at[sem], {"row": to})

    @functools.cache
    def c_hop(way, s, c):
        step = side(way)
        piece = x_buf.at[pl.ds(8 * c, 8), tile_cols(col_at(-step * (s - 1)))]
        sem = (way * 2 + s - 1) * 2 + c
        return remote(piece, piece, c_send.at[sem], c_recv.at[sem], {"col": col_at(step)})

    @functools.cache
    def z_hop(way):
        src = x_buf.at[pl.ds(13 if way == 0 else 0, 3), tile_cols(q)]
        dst = x_edge.at[pl.ds(3 * way, 3), tile_cols(q)]
        return remote(src, dst, z_send.at[way], z_recv.at[way], {"row": row_at(side(way))})

    @functools.cache
    def h_hop(d):
        piece = x_edge.at[:, tile_cols(q)]
        return remote(piece, piece, h_send.at[d - 1], h_recv.at[d - 1], {"col": col_at(d)})

    def chunk(way, k):
        return k if way == 0 else 1 - k

    in_c.wait()
    for way in range(2):
        start(c_hop(way, 1, way))
        start(f_hop(way, 1))
    for way in range(2):
        start(z_hop(way))
    for way in range(2):
        start(c_hop(way, 1, 1 - way))

    in_i.wait()
    n = lax.broadcasted_iota(jnp.int32, (64, 128), 0)
    lane = lax.broadcasted_iota(jnp.int32, (64, 128), 1)
    band = (4 * half + ((n >> 2) & 3)) * 16 + (n >> 4) * 4 + (n & 3)
    pick = jnp.where(lane == band, 1.0, 0.0).astype(BF16)
    picked = lax.dot_general(
        pick, img_in[...].reshape(32, 128), (((1,), (1,)), ((), ())), preferred_element_type=F32
    ).astype(BF16)
    n = lax.broadcasted_iota(jnp.int32, (32, 128), 0)
    lane = lax.broadcasted_iota(jnp.int32, (32, 128), 1)
    place = jnp.where(lane == (n >> 4) * 64 + q * 16 + (n & 15), 1.0, 0.0).astype(BF16)
    img_out[...] = jnp.dot(picked, place, preferred_element_type=F32).astype(BF16).reshape(COLS, 16, 128)

    for way in range(2):
        z_hop(way).wait_recv()
    for d in (1, 3, 2):
        start(h_hop(d))
    for way in range(2):
        c_hop(way, 1, way).wait_recv()
        start(c_hop(way, 2, way))
    for way in range(2):
        f_hop(way, 1).wait_recv()
        start(f_hop(way, 3))
        start(f_hop(way, 2))
    for way in range(2):
        start(f_hop(way, 0))
    v = lax.broadcasted_iota(jnp.int32, (64, 128), 0)

    def shift_codes(x, at):
        x = x.astype(F32)
        for b in range(TAPS):
            s = b - 3
            moved = x if s == 0 else pltpu.roll(x, (-s) % 64, 0)
            if s:
                moved = jnp.where((v + s >= 0) & (v + s < 64), moved, 0.0)
            x7[pl.ds(pl.multiple_of(at * 64, 64), 64), b * 128 : (b + 1) * 128] = moved.astype(BF16)

    def shift_tile(u, carry):
        shift_codes(x_buf[u], u + 3)
        return carry

    def shift_edge(e, carry):
        x = x_edge[e]
        inside = jnp.where(e < 3, r, ROWS - 1 - r) > 0
        shift_codes(jnp.where(inside, x, jnp.zeros_like(x)), jnp.where(e < 3, e, e + 16))
        return carry

    for d in range(1, COLS):
        h_hop(d).wait_recv()
    lax.fori_loop(0, 6, shift_edge, 0)
    for way in range(2):
        c_hop(way, 1, 1 - way).wait_recv()
    c_hop(0, 2, 0).wait_recv()
    lax.fori_loop(0, 8, shift_tile, 0)
    c_hop(1, 2, 1).wait_recv()
    lax.fori_loop(8, 16, shift_tile, 0)
    for way in range(2):
        for kind in (0, 2, 3):
            f_hop(way, kind).wait_recv()

    i_copies = []
    for d in range(1, COLS):
        to = col_at(d)
        i_copies.append(
            start(remote(img_out.at[to], img_got.at[d - 1], i_send.at[d - 1], i_recv.at[d - 1], {"col": to}))
        )

    product = lax.dot_general(
        f_buf[...].reshape(256, 896), x7[...], (((1,), (1,)), ((), ())), preferred_element_type=F32
    )
    pt[...] = product.reshape(8, 4, 8, 1408)

    lane = lax.broadcasted_iota(jnp.int32, (32, 128), 1)
    low = lax.broadcasted_iota(jnp.int32, (4, 8, 128), 1) < 4

    def swapped(x):
        return pltpu.roll(x, 64, 1)

    def turned(x):
        return pltpu.roll(x, 4, 1)

    def tap_sums(j):
        total = None
        for m in range(4):
            if j + m < 11:
                term = pt[:, m, :, (j + m) * 128 : (j + m + 1) * 128]
                total = term if total is None else total + term
        total = total.reshape(4, 2, 8, 128)
        one, two = total[:, 0], total[:, 1]
        even = jnp.where(low, one, turned(two)).reshape(32, 128)
        odd = jnp.where(low, turned(one), two).reshape(32, 128)
        return even, swapped(odd)

    even, odd = tap_sums(0)
    for p in range(8):
        next_even, next_odd = tap_sums(p + 1)
        value = even + jnp.where(lane < 64, odd, next_odd)
        part_out[2 * p] = value[:16].astype(BF16)
        part_out[2 * p + 1] = value[16:].astype(BF16)
        even, odd = next_even, next_odd
    p_copies = []
    for d in range(1, ATOMS):
        to = lax.rem(t + d, ATOMS)
        p_copies.append(
            start(remote(part_out.at[to], part_got.at[d - 1], p_send.at[d - 1], p_recv.at[d - 1], {"atom": to}))
        )
    for copy in i_copies:
        copy.wait_recv()
    own_image = img_out[q].astype(F32)
    for d in range(COLS - 1):
        own_image = own_image + img_got[d].astype(F32)
    synth = part_out[t].astype(F32)
    for copy in p_copies:
        copy.wait_recv()
    for d in range(ATOMS - 1):
        synth = synth + part_got[d].astype(F32)
    resid[t] = (synth - own_image).astype(BF16)
    r_copies = []
    for d in range(1, ATOMS):
        to = lax.rem(t + d, ATOMS)
        r_copies.append(
            start(remote(resid.at[t], resid.at[t], r_send.at[d - 1], r_recv.at[d - 1], {"atom": to}))
        )
    for copy in r_copies:
        copy.wait_recv()
    e_copies = [
        start(remote(resid.at[pl.ds(0, 4)], edge_got.at[1], e_send.at[0], e_recv.at[0], {"row": row_at(-1)})),
        start(remote(resid.at[pl.ds(12, 4)], edge_got.at[0], e_send.at[1], e_recv.at[1], {"row": row_at(1)})),
    ]

    def tile_of(ref, p):
        return jnp.concatenate([ref[2 * p], ref[2 * p + 1]], axis=0).astype(F32)

    tiles = {2 + p: tile_of(resid, p) for p in range(8)}
    flipped = {j: swapped(tiles[j]) for j in range(2, 10)}
    zero = jnp.zeros((32, 128), F32)

    def paired(even, odd):
        even, odd = even.reshape(4, 8, 128), odd.reshape(4, 8, 128)
        one, two = jnp.where(low, even, turned(odd)), jnp.where(low, turned(even), odd)
        return jnp.stack([one, two], axis=1).reshape(8, 8, 128)

    shares = [
        paired(tiles.get(j + 2, zero), jnp.where(lane < 64, flipped.get(j + 1, zero), flipped.get(j + 2, zero)))
        if j < 8 else paired(zero, jnp.where(lane < 64, flipped[9], zero))
        for j in range(9)
    ]
    none = jnp.zeros((8, 8, 128), F32)
    for j in range(11):
        taps = [shares[j - m] if 0 <= j - m < 9 else none for m in range(4)]
        xrg[:, j * 128 : (j + 1) * 128] = jnp.stack(taps, axis=1).reshape(256, 128).astype(BF16)

    grad = jnp.dot(xrg[...], x7[...], preferred_element_type=F32)
    g_out[...] = grad.astype(BF16).reshape(ROWS, 32, 896)

    @functools.cache
    def g_hop(way, kind):
        step, sem = side(way), way * 4 + kind
        rows = pl.ds(16 * way, 16) if kind == 1 else slice(None)
        src = g_sum.at[way] if kind == 3 else g_out.at[row_at(step * (3, 4, 1)[kind]), rows]
        to = row_at(step if kind in (0, 2) else 2 * step)
        return remote(src, g_got.at[way, kind, rows], g_send.at[sem], g_recv.at[sem], {"row": to})

    def g_relay():
        for way in range(2):
            g_hop(way, 0).wait_recv()
            g_hop(way, 1).wait_recv()
            dest = row_at(2 * side(way))
            term = g_out[dest].astype(F32) + g_got[way, 0].astype(F32)
            near = slice(16 * way, 16 * way + 16)
            far = slice(16 - 16 * way, 32 - 16 * way)
            g_sum[way, near, :] = (term[near] + g_got[way, 1, near, :].astype(F32)).astype(BF16)
            g_sum[way, far, :] = term[far].astype(BF16)
            start(g_hop(way, 3))

    for kind in range(2):
        for way in range(2):
            start(g_hop(way, kind))

    both = {}

    def rows_of_taps(slot, j):
        for at in range(j, j + 4):
            if at not in both:
                both[at] = paired(jnp.where(lane < 64, flipped[at], flipped[at + 1]), tiles[at])
        tap_rows = jnp.stack([both[j + 3 - m] for m in range(4)], axis=1).reshape(256, 128)
        xrb[:, slot * 128 : (slot + 1) * 128] = tap_rows.astype(BF16)

    for slot in range(4):
        rows_of_taps(slot, slot + 2)

    def back_part(at):
        cols = slice(at * 512, (at + 1) * 512)
        p2[...] = lax.dot_general(
            xrb[:, cols], f_buf[...].reshape(256, 896), (((0,), (0,)), ((), ())), preferred_element_type=F32
        )

        def shift_back(u, carry):
            here = pl.ds(pl.multiple_of(u * 64, 64), 64)
            total = p2[here, 384:512]
            for b in range(TAPS):
                s = b - 3
                if s:
                    moved = pltpu.roll(p2[here, b * 128 : (b + 1) * 128], s % 64, 0)
                    total = total + jnp.where((v - s >= 0) & (v - s < 64), moved, 0.0)
            bk_out[at * 8 + u] = total.astype(BF16)
            return carry

        lax.fori_loop(0, 8, shift_back, 0)

    @functools.cache
    def b_hop(way, s, c):
        step = side(way)
        rows = pl.ds(8 * c, 8)
        alone = s == 2 or way == 1 or c == 1
        src = bk_out.at[rows, tile_cols(col_at(step * s))] if alone else bk_sum
        sem = (way * 2 + s - 1) * 2 + c
        to = col_at(2 if way == 1 and s == 2 else step)
        return remote(src, bk_got.at[way, s - 1, rows], b_send.at[sem], b_recv.at[sem], {"col": to})

    def b_step():
        b_hop(0, 2, 0).wait_recv()
        own = bk_out[0:8, tile_cols(col_at(1)), :].astype(F32)
        bk_sum[...] = (own + bk_got[0, 1, 0:8].astype(F32)).astype(BF16)
        start(b_hop(0, 1, 0))

    back_part(0)
    start(b_hop(0, 2, 0))
    start(b_hop(1, 1, 0))
    not_first = jnp.where(r > 0, 1.0, 0.0).astype(F32)
    not_last = jnp.where(r < ROWS - 1, 1.0, 0.0).astype(F32)
    for copy in e_copies:
        copy.wait_recv()
    for at in range(2):
        tiles[at] = not_first * tile_of(edge_got.at[0], at)
        tiles[10 + at] = not_last * tile_of(edge_got.at[1], at)
        flipped[at] = swapped(tiles[at])
        flipped[10 + at] = swapped(tiles[10 + at])
    for slot, j in enumerate((0, 1, 6, 7)):
        rows_of_taps(4 + slot, j)
    back_part(1)
    start(b_hop(1, 2, 1))
    start(b_hop(0, 1, 1))
    start(b_hop(1, 1, 1))
    b_step()
    g_relay()
    for way in range(2):
        start(g_hop(way, 2))
    for way in range(2):
        for c in range(2):
            b_hop(way, 1, c).wait_recv()
    b_hop(1, 2, 1).wait_recv()

    def shrink(far, at, carry):
        u = jnp.where(at < 8, at + 4, jnp.where(at < 12, at - 8, at))
        back = bk_out[at, tile_cols(q)].astype(F32)
        for way in range(2):
            back = back + bk_got[way, 0, at].astype(F32)
        if far:
            back = back + bk_got[1, 1, at].astype(F32)
        moved = x_buf[u, tile_cols(q)].astype(F32) - 0.05 * back
        out_codes[u] = (moved - jnp.clip(moved, -0.02, 0.02)).astype(BF16)
        return carry

    lax.fori_loop(0, 8, functools.partial(shrink, False), 0)
    lax.fori_loop(8, 16, functools.partial(shrink, True), 0)

    for way in range(2):
        for kind in (2, 3):
            g_hop(way, kind).wait_recv()
    for b in range(TAPS):
        cols = slice(b * 128, (b + 1) * 128)
        total = g_out[r, :, cols].astype(F32)
        for way in range(2):
            for kind in (2, 3):
                total = total + g_got[way, kind, :, cols].astype(F32)
        for a in range(TAPS):
            out_grad[a * TAPS + b] = total[4 * a : 4 * a + 4]

    for copy in started:
        copy.wait_send()


def adam_update(master, moment, second, grad):
    new_moment = 0.9 * moment + 0.1 * grad
    new_second = 0.999 * second + 0.001 * grad * grad
    new_dictionary = master - 0.05 * (new_moment / first_fix) / (
        jnp.sqrt(new_second / second_fix) + 1e-08
    )
    return (new_dictionary, new_moment, new_second)


def local(codes, image, master, moment, second):
    dma = pltpu.SemaphoreType.DMA
    vmem = pltpu.VMEM
    hbm_spec = pl.BlockSpec(memory_space=pltpu.HBM)
    vmem_spec = pl.BlockSpec(memory_space=vmem)
    bands = master.shape[0]
    taps = TAPS * TAPS
    new_codes, grad = pl.pallas_call(
        kernel,
        out_shape=(
            jax.ShapeDtypeStruct(codes.shape, BF16),
            jax.ShapeDtypeStruct((taps, bands, 128), F32),
        ),
        in_specs=[hbm_spec] * 3,
        out_specs=(vmem_spec,) * 2,
        scratch_shapes=[
            vmem((16, 64, 128), BF16),
            vmem((6, 64, 128), BF16),
            vmem((1408, 896), BF16),
            vmem((8, 32, 896), BF16),
            vmem((taps, bands, 128), F32),
            vmem((2, 16, 128), BF16),
            vmem((4, 16, 128), BF16),
            vmem((3, 16, 128), BF16),
            vmem((8, 4, 8, 1408), F32),
            vmem((16, 16, 128), BF16),
            vmem((15, 16, 128), BF16),
            vmem((16, 16, 128), BF16),
            vmem((2, 4, 16, 128), BF16),
            vmem((256, 1408), BF16),
            vmem((256, 1024), BF16),
            vmem((8, 32, 896), BF16),
            vmem((2, 32, 896), BF16),
            vmem((2, 4, 32, 896), BF16),
            vmem((512, 896), F32),
            vmem((16, 64, 128), BF16),
            vmem((8, 16, 128), BF16),
            vmem((2, 2, 16, 16, 128), BF16),
            dma((3,)),
            dma((8,)), dma((8,)), dma((8,)), dma((8,)), dma((3,)), dma((3,)),
            dma((2,)), dma((2,)), dma((3,)), dma((3,)), dma((15,)), dma((15,)), dma((15,)), dma((15,)), dma((2,)), dma((2,)),
            dma((8,)), dma((8,)), dma((8,)), dma((8,)),
        ],
        compiler_params=pltpu.CompilerParams(
            collective_id=0, has_side_effects=True, vmem_limit_bytes=60 * 1024 * 1024
        ),
        name="dictionary_step",
    )(codes, image, jnp.transpose(master, (1, 2, 0, 3)).reshape(taps, bands, 128))
    grad = jnp.transpose(grad.reshape(TAPS, TAPS, bands, 128), (2, 0, 1, 3))
    return (new_codes, *adam_update(master, moment, second, grad))


def solution(mesh):
    tile = P("row", "col", "atom")
    bank = P(("row", "col"), None, None, "atom")
    return jax.shard_map(
        local,
        mesh=mesh,
        in_specs=(tile, P("row", "col", None), bank, bank, bank),
        out_specs=(tile, bank, bank, bank),
        check_vma=False,
    )
```

```python
import functools

import jax
import jax.numpy as jnp
from jax import lax
from jax.experimental import pallas as pl
from jax.experimental.pallas import tpu as pltpu
from jax.sharding import PartitionSpec as P

MESH = pl.DeviceIdType.MESH
F32, BF16 = jnp.float32, jnp.bfloat16
first_fix = 0.9999734386011124
second_fix = 0.09520785288629038
ROWS, COLS, ATOMS = 8, 4, 16
TAPS = 7


def kernel(
    codes, image, master,
    out_codes, out_grad,
    x_buf, x_edge, x7, f_buf, m_buf,
    img_in, img_out, img_got,
    pt, part_out, part_got,
    resid, edge_got, xrg, xrb,
    g_out, g_sum, g_got, p2, bk_out, bk_sum, bk_got,
    in_sem, f_send, f_recv, c_send, c_recv, i_send, i_recv,
    z_send, z_recv, h_send, h_recv, p_send, p_recv, r_send, r_recv, e_send, e_recv,
    g_send, g_recv, b_send, b_recv,
):
    r = lax.axis_index("row")
    q = lax.axis_index("col")
    t = lax.axis_index("atom")
    pair, half = t // 2, lax.rem(t, 2)
    started = []

    def start(copy):
        copy.start()
        started.append(copy)
        return copy

    def remote(src, dst, send, recv, who):
        return pltpu.make_async_remote_copy(
            src_ref=src, dst_ref=dst, send_sem=send, recv_sem=recv,
            device_id=who, device_id_type=MESH,
        )

    def row_at(d):
        return lax.rem(r + d + 2 * ROWS, ROWS)

    def col_at(d):
        return lax.rem(q + d + 2 * COLS, COLS)

    def tile_cols(at):
        return pl.ds(pl.multiple_of(at * 16, 16), 16)

    in_m = pltpu.make_async_copy(master, m_buf, in_sem.at[0])
    in_c = pltpu.make_async_copy(codes, x_buf.at[:, tile_cols(q)], in_sem.at[1])
    in_i = pltpu.make_async_copy(image.at[pl.ds(2 * pair, 2)], img_in, in_sem.at[2])
    for copy in (in_m, in_c, in_i):
        copy.start()

    barrier = pltpu.get_barrier_semaphore()
    peers = [{"row": row_at(d)} for d in (1, -1, 2, -2)]
    peers += [{"col": col_at(d)} for d in range(1, COLS)]
    peers += [{"atom": lax.rem(t + d, ATOMS)} for d in range(1, ATOMS)]
    for who in peers:
        pl.semaphore_signal(barrier, inc=1, device_id=who, device_id_type=MESH)

    in_m.wait()
    for b in range(TAPS):
        rows = [m_buf[a * TAPS + b] for a in range(TAPS)] + [jnp.zeros((4, 128), F32)]
        f_buf[r, :, b * 128 : (b + 1) * 128] = jnp.concatenate(rows, axis=0).astype(BF16)

    pl.semaphore_wait(barrier, len(peers))

    def side(way):
        return 1 if way == 0 else -1

    @functools.cache
    def f_hop(way, kind):
        step, sem = side(way), way * 4 + kind
        rows = pl.ds(16 * way, 16) if kind == 3 else slice(None)
        piece = f_buf.at[r if kind < 2 else row_at(-2 * step), rows]
        to = row_at(step if kind in (0, 2) else 2 * step)
        return remote(piece, piece, f_send.at[sem], f_recv.at[sem], {"row": to})

    @functools.cache
    def c_hop(way, s, c):
        step = side(way)
        piece = x_buf.at[pl.ds(8 * c, 8), tile_cols(col_at(-step * (s - 1)))]
        sem = (way * 2 + s - 1) * 2 + c
        return remote(piece, piece, c_send.at[sem], c_recv.at[sem], {"col": col_at(step)})

    @functools.cache
    def z_hop(way):
        src = x_buf.at[pl.ds(13 if way == 0 else 0, 3), tile_cols(q)]
        dst = x_edge.at[pl.ds(3 * way, 3), tile_cols(q)]
        return remote(src, dst, z_send.at[way], z_recv.at[way], {"row": row_at(side(way))})

    @functools.cache
    def h_hop(d):
        piece = x_edge.at[:, tile_cols(q)]
        return remote(piece, piece, h_send.at[d - 1], h_recv.at[d - 1], {"col": col_at(d)})

    def chunk(way, k):
        return k if way == 0 else 1 - k

    in_c.wait()
    for way in range(2):
        start(c_hop(way, 1, way))
        start(f_hop(way, 1))
    for way in range(2):
        start(z_hop(way))
    for way in range(2):
        start(c_hop(way, 1, 1 - way))

    in_i.wait()
    n = lax.broadcasted_iota(jnp.int32, (64, 128), 0)
    lane = lax.broadcasted_iota(jnp.int32, (64, 128), 1)
    band = (4 * half + ((n >> 2) & 3)) * 16 + (n >> 4) * 4 + (n & 3)
    pick = jnp.where(lane == band, 1.0, 0.0).astype(BF16)
    picked = lax.dot_general(
        pick, img_in[...].reshape(32, 128), (((1,), (1,)), ((), ())), preferred_element_type=F32
    ).astype(BF16)
    n = lax.broadcasted_iota(jnp.int32, (32, 128), 0)
    lane = lax.broadcasted_iota(jnp.int32, (32, 128), 1)
    place = jnp.where(lane == (n >> 4) * 64 + q * 16 + (n & 15), 1.0, 0.0).astype(BF16)
    img_out[...] = jnp.dot(picked, place, preferred_element_type=F32).astype(BF16).reshape(COLS, 16, 128)

    for way in range(2):
        z_hop(way).wait_recv()
    for d in (1, 3, 2):
        start(h_hop(d))
    for way in range(2):
        c_hop(way, 1, way).wait_recv()
        start(c_hop(way, 2, way))
    for way in range(2):
        f_hop(way, 1).wait_recv()
        start(f_hop(way, 3))
        start(f_hop(way, 2))
    for way in range(2):
        start(f_hop(way, 0))
    v = lax.broadcasted_iota(jnp.int32, (64, 128), 0)

    def shift_codes(x, at):
        x = x.astype(F32)
        for b in range(TAPS):
            s = b - 3
            moved = x if s == 0 else pltpu.roll(x, (-s) % 64, 0)
            if s:
                moved = jnp.where((v + s >= 0) & (v + s < 64), moved, 0.0)
            x7[pl.ds(pl.multiple_of(at * 64, 64), 64), b * 128 : (b + 1) * 128] = moved.astype(BF16)

    def shift_tile(u, carry):
        shift_codes(x_buf[u], u + 3)
        return carry

    def shift_edge(e, carry):
        x = x_edge[e]
        inside = jnp.where(e < 3, r, ROWS - 1 - r) > 0
        shift_codes(jnp.where(inside, x, jnp.zeros_like(x)), jnp.where(e < 3, e, e + 16))
        return carry

    for d in range(1, COLS):
        h_hop(d).wait_recv()
    lax.fori_loop(0, 6, shift_edge, 0)
    for way in range(2):
        c_hop(way, 1, 1 - way).wait_recv()
    c_hop(0, 2, 0).wait_recv()
    lax.fori_loop(0, 8, shift_tile, 0)
    c_hop(1, 2, 1).wait_recv()
    lax.fori_loop(8, 16, shift_tile, 0)
    for way in range(2):
        for kind in (0, 2, 3):
            f_hop(way, kind).wait_recv()

    i_copies = []
    for d in range(1, COLS):
        to = col_at(d)
        i_copies.append(
            start(remote(img_out.at[to], img_got.at[d - 1], i_send.at[d - 1], i_recv.at[d - 1], {"col": to}))
        )

    product = lax.dot_general(
        f_buf[...].reshape(256, 896), x7[...], (((1,), (1,)), ((), ())), preferred_element_type=F32
    )
    pt[...] = product.reshape(8, 4, 8, 1408)

    lane = lax.broadcasted_iota(jnp.int32, (32, 128), 1)
    low = lax.broadcasted_iota(jnp.int32, (4, 8, 128), 1) < 4

    def swapped(x):
        return pltpu.roll(x, 64, 1)

    def turned(x):
        return pltpu.roll(x, 4, 1)

    def tap_sums(j):
        total = None
        for m in range(4):
            if j + m < 11:
                term = pt[:, m, :, (j + m) * 128 : (j + m + 1) * 128]
                total = term if total is None else total + term
        total = total.reshape(4, 2, 8, 128)
        one, two = total[:, 0], total[:, 1]
        even = jnp.where(low, one, turned(two)).reshape(32, 128)
        odd = jnp.where(low, turned(one), two).reshape(32, 128)
        return even, swapped(odd)

    even, odd = tap_sums(0)
    for p in range(8):
        next_even, next_odd = tap_sums(p + 1)
        value = even + jnp.where(lane < 64, odd, next_odd)
        part_out[2 * p] = value[:16].astype(BF16)
        part_out[2 * p + 1] = value[16:].astype(BF16)
        even, odd = next_even, next_odd
    p_copies = []
    for d in range(1, ATOMS):
        to = lax.rem(t + d, ATOMS)
        p_copies.append(
            start(remote(part_out.at[to], part_got.at[d - 1], p_send.at[d - 1], p_recv.at[d - 1], {"atom": to}))
        )
    for copy in i_copies:
        copy.wait_recv()
    own_image = img_out[q].astype(F32)
    for d in range(COLS - 1):
        own_image = own_image + img_got[d].astype(F32)
    synth = part_out[t].astype(F32)
    for copy in p_copies:
        copy.wait_recv()
    for d in range(ATOMS - 1):
        synth = synth + part_got[d].astype(F32)
    resid[t] = (synth - own_image).astype(BF16)
    r_copies = []
    for d in range(1, ATOMS):
        to = lax.rem(t + d, ATOMS)
        r_copies.append(
            start(remote(resid.at[t], resid.at[t], r_send.at[d - 1], r_recv.at[d - 1], {"atom": to}))
        )
    for copy in r_copies:
        copy.wait_recv()
    e_copies = [
        start(remote(resid.at[pl.ds(0, 4)], edge_got.at[1], e_send.at[0], e_recv.at[0], {"row": row_at(-1)})),
        start(remote(resid.at[pl.ds(12, 4)], edge_got.at[0], e_send.at[1], e_recv.at[1], {"row": row_at(1)})),
    ]

    def tile_of(ref, p):
        return jnp.concatenate([ref[2 * p], ref[2 * p + 1]], axis=0).astype(F32)

    tiles = {2 + p: tile_of(resid, p) for p in range(8)}
    flipped = {j: swapped(tiles[j]) for j in range(2, 10)}
    zero = jnp.zeros((32, 128), F32)

    def paired(even, odd):
        even, odd = even.reshape(4, 8, 128), odd.reshape(4, 8, 128)
        one, two = jnp.where(low, even, turned(odd)), jnp.where(low, turned(even), odd)
        return jnp.stack([one, two], axis=1).reshape(8, 8, 128)

    shares = [
        paired(tiles.get(j + 2, zero), jnp.where(lane < 64, flipped.get(j + 1, zero), flipped.get(j + 2, zero)))
        if j < 8 else paired(zero, jnp.where(lane < 64, flipped[9], zero))
        for j in range(9)
    ]
    none = jnp.zeros((8, 8, 128), F32)
    for j in range(11):
        taps = [shares[j - m] if 0 <= j - m < 9 else none for m in range(4)]
        xrg[:, j * 128 : (j + 1) * 128] = jnp.stack(taps, axis=1).reshape(256, 128).astype(BF16)

    grad = jnp.dot(xrg[...], x7[...], preferred_element_type=F32)
    g_out[...] = grad.astype(BF16).reshape(ROWS, 32, 896)

    @functools.cache
    def g_hop(way, kind):
        step, sem = side(way), way * 4 + kind
        rows = pl.ds(16 * way, 16) if kind == 1 else slice(None)
        src = g_sum.at[way] if kind == 3 else g_out.at[row_at(step * (3, 4, 1)[kind]), rows]
        to = row_at(step if kind in (0, 2) else 2 * step)
        return remote(src, g_got.at[way, kind, rows], g_send.at[sem], g_recv.at[sem], {"row": to})

    def g_relay():
        for way in range(2):
            g_hop(way, 0).wait_recv()
            g_hop(way, 1).wait_recv()
            dest = row_at(2 * side(way))
            term = g_out[dest].astype(F32) + g_got[way, 0].astype(F32)
            near = slice(16 * way, 16 * way + 16)
            far = slice(16 - 16 * way, 32 - 16 * way)
            g_sum[way, near, :] = (term[near] + g_got[way, 1, near, :].astype(F32)).astype(BF16)
            g_sum[way, far, :] = term[far].astype(BF16)
            start(g_hop(way, 3))

    for kind in range(2):
        for way in range(2):
            start(g_hop(way, kind))

    both = {}

    def rows_of_taps(slot, j):
        for at in range(j, j + 4):
            if at not in both:
                both[at] = paired(jnp.where(lane < 64, flipped[at], flipped[at + 1]), tiles[at])
        tap_rows = jnp.stack([both[j + 3 - m] for m in range(4)], axis=1).reshape(256, 128)
        xrb[:, slot * 128 : (slot + 1) * 128] = tap_rows.astype(BF16)

    for slot in range(4):
        rows_of_taps(slot, slot + 2)

    def back_part(at):
        cols = slice(at * 512, (at + 1) * 512)
        p2[...] = lax.dot_general(
            xrb[:, cols], f_buf[...].reshape(256, 896), (((0,), (0,)), ((), ())), preferred_element_type=F32
        )

        def shift_back(u, carry):
            here = pl.ds(pl.multiple_of(u * 64, 64), 64)
            total = p2[here, 384:512]
            for b in range(TAPS):
                s = b - 3
                if s:
                    moved = pltpu.roll(p2[here, b * 128 : (b + 1) * 128], s % 64, 0)
                    total = total + jnp.where((v - s >= 0) & (v - s < 64), moved, 0.0)
            bk_out[at * 8 + u] = total.astype(BF16)
            return carry

        lax.fori_loop(0, 8, shift_back, 0)

    @functools.cache
    def b_hop(way, s, c):
        step = side(way)
        rows = pl.ds(8 * c, 8)
        alone = s == 2 or way == 1 or c == 1
        src = bk_out.at[rows, tile_cols(col_at(step * s))] if alone else bk_sum
        sem = (way * 2 + s - 1) * 2 + c
        to = col_at(2 if way == 1 and s == 2 else step)
        return remote(src, bk_got.at[way, s - 1, rows], b_send.at[sem], b_recv.at[sem], {"col": to})

    def b_step():
        b_hop(0, 2, 0).wait_recv()
        own = bk_out[0:8, tile_cols(col_at(1)), :].astype(F32)
        bk_sum[...] = (own + bk_got[0, 1, 0:8].astype(F32)).astype(BF16)
        start(b_hop(0, 1, 0))

    back_part(0)
    start(b_hop(0, 2, 0))
    start(b_hop(1, 1, 0))
    not_first = jnp.where(r > 0, 1.0, 0.0).astype(F32)
    not_last = jnp.where(r < ROWS - 1, 1.0, 0.0).astype(F32)
    for copy in e_copies:
        copy.wait_recv()
    for at in range(2):
        tiles[at] = not_first * tile_of(edge_got.at[0], at)
        tiles[10 + at] = not_last * tile_of(edge_got.at[1], at)
        flipped[at] = swapped(tiles[at])
        flipped[10 + at] = swapped(tiles[10 + at])
    for slot, j in enumerate((0, 1, 6, 7)):
        rows_of_taps(4 + slot, j)
    back_part(1)
    start(b_hop(1, 2, 1))
    start(b_hop(0, 1, 1))
    start(b_hop(1, 1, 1))
    for way in range(2):
        start(g_hop(way, 2))
    b_step()
    g_relay()
    for way in range(2):
        for c in range(2):
            b_hop(way, 1, c).wait_recv()
    b_hop(1, 2, 1).wait_recv()

    def shrink(far, at, carry):
        u = jnp.where(at < 8, at + 4, jnp.where(at < 12, at - 8, at))
        back = bk_out[at, tile_cols(q)].astype(F32)
        for way in range(2):
            back = back + bk_got[way, 0, at].astype(F32)
        if far:
            back = back + bk_got[1, 1, at].astype(F32)
        moved = x_buf[u, tile_cols(q)].astype(F32) - 0.05 * back
        out_codes[u] = (moved - jnp.clip(moved, -0.02, 0.02)).astype(BF16)
        return carry

    lax.fori_loop(0, 8, functools.partial(shrink, False), 0)
    lax.fori_loop(8, 16, functools.partial(shrink, True), 0)

    for way in range(2):
        for kind in (2, 3):
            g_hop(way, kind).wait_recv()
    for b in range(TAPS):
        cols = slice(b * 128, (b + 1) * 128)
        total = g_out[r, :, cols].astype(F32)
        for way in range(2):
            for kind in (2, 3):
                total = total + g_got[way, kind, :, cols].astype(F32)
        for a in range(TAPS):
            out_grad[a * TAPS + b] = total[4 * a : 4 * a + 4]

    for copy in started:
        copy.wait_send()


def adam_update(master, moment, second, grad):
    new_moment = 0.9 * moment + 0.1 * grad
    new_second = 0.999 * second + 0.001 * grad * grad
    new_dictionary = master - 0.05 * (new_moment / first_fix) / (
        jnp.sqrt(new_second / second_fix) + 1e-08
    )
    return (new_dictionary, new_moment, new_second)


def local(codes, image, master, moment, second):
    dma = pltpu.SemaphoreType.DMA
    vmem = pltpu.VMEM
    hbm_spec = pl.BlockSpec(memory_space=pltpu.HBM)
    vmem_spec = pl.BlockSpec(memory_space=vmem)
    bands = master.shape[0]
    taps = TAPS * TAPS
    new_codes, grad = pl.pallas_call(
        kernel,
        out_shape=(
            jax.ShapeDtypeStruct(codes.shape, BF16),
            jax.ShapeDtypeStruct((taps, bands, 128), F32),
        ),
        in_specs=[hbm_spec] * 3,
        out_specs=(vmem_spec,) * 2,
        scratch_shapes=[
            vmem((16, 64, 128), BF16),
            vmem((6, 64, 128), BF16),
            vmem((1408, 896), BF16),
            vmem((8, 32, 896), BF16),
            vmem((taps, bands, 128), F32),
            vmem((2, 16, 128), BF16),
            vmem((4, 16, 128), BF16),
            vmem((3, 16, 128), BF16),
            vmem((8, 4, 8, 1408), F32),
            vmem((16, 16, 128), BF16),
            vmem((15, 16, 128), BF16),
            vmem((16, 16, 128), BF16),
            vmem((2, 4, 16, 128), BF16),
            vmem((256, 1408), BF16),
            vmem((256, 1024), BF16),
            vmem((8, 32, 896), BF16),
            vmem((2, 32, 896), BF16),
            vmem((2, 4, 32, 896), BF16),
            vmem((512, 896), F32),
            vmem((16, 64, 128), BF16),
            vmem((8, 16, 128), BF16),
            vmem((2, 2, 16, 16, 128), BF16),
            dma((3,)),
            dma((8,)), dma((8,)), dma((8,)), dma((8,)), dma((3,)), dma((3,)),
            dma((2,)), dma((2,)), dma((3,)), dma((3,)), dma((15,)), dma((15,)), dma((15,)), dma((15,)), dma((2,)), dma((2,)),
            dma((8,)), dma((8,)), dma((8,)), dma((8,)),
        ],
        compiler_params=pltpu.CompilerParams(
            collective_id=0, has_side_effects=True, vmem_limit_bytes=60 * 1024 * 1024
        ),
        name="dictionary_step",
    )(codes, image, jnp.transpose(master, (1, 2, 0, 3)).reshape(taps, bands, 128))
    grad = jnp.transpose(grad.reshape(TAPS, TAPS, bands, 128), (2, 0, 1, 3))
    return (new_codes, *adam_update(master, moment, second, grad))


def solution(mesh):
    tile = P("row", "col", "atom")
    bank = P(("row", "col"), None, None, "atom")
    return jax.shard_map(
        local,
        mesh=mesh,
        in_specs=(tile, P("row", "col", None), bank, bank, bank),
        out_specs=(tile, bank, bank, bank),
        check_vma=False,
    )
```
